256 devices in a mesh: elem: 64 (over z, y, core), sec: 4 (over x).
Axes of the slice: x: 4, y: 4, z: 8, core: 2. Of those that a mesh axis runs over, the one named last changes fastest.
Arguments:
- fields: float32 [8192, 16, 640], P(('elem', 'sec')), may hold values from -6 to 6
- neighbours: int32 [8192, 4], P(('elem', 'sec')), may hold values from 0 to 8191, as said below
- operator: float32 [16, 16], replicated, may hold values from -1.5 to 1.5
- rates: float32 [640], replicated, may hold values from 0.05 to 0.5
- regime_ids: int32 [131072, 1], P(('elem', 'sec')), may hold values from 0 to 63; in each aligned block of 512 rows (0 to 511, 512 to 1023, ...) at most 16 rows name the same one
- input_proj: bfloat16 [64, 640, 1024], P('elem', None, 'sec'), may hold values from -0.4375 to 0.4375
- hidden_proj: bfloat16 [64, 2, 1024, 1024], P('elem', None, None, 'sec'), may hold values from -0.25 to 0.25
- output_proj: bfloat16 [64, 1024, 640], P('elem', None, 'sec'), may hold values from -0.25 to 0.25
Outputs:
- updated: float32 [8192, 16, 640], P(('elem', 'sec'))
The draws below stay inside these ranges and needn't reach their ends.
Inputs may be any that keep to these rules, and one draw needn't show every extreme that they name: If edge k of element a names b, the opposite edge (west with east, south with north) of b names a. West and east neighbours are among the 32 elements of the same device along elem+sec, where element g lies on device g // 32; south neighbours lie on the device before and north neighbours on the device after, wrapping around. `regime_ids`: of the 512 columns of one device, at most 16 name the same regime, and some device reaches that.
All inputs are finite; a program needn't handle non-finite values.
Results may differ from the reference program's by a relative error of at most 0.015.
Values may be sent and summed in bfloat16 or wider, within the bound.
No kernel may reach another device: no remote copies, remote signals or barrier semaphores. Data moves between devices by JAX's collectives and lax.ppermute only.
A program may use at most 64 MiB of HBM per device.

```python
import math
import jax
import jax.numpy as jnp
import numpy as np
from jax import lax

E_DEV = 32
POINTS = 16
HID = 1024
MID = 2
DYN_STEPS = 2
F = 640
ELEMS = 8192
COLS_DEV = 512
COLS = 131072
REGIMES = 64
CAP = 16
DEVICES = 256


def draw_neighbours(key, part):
    groups = ELEMS // E_DEV
    key_row, key_col = jax.random.split(jax.random.fold_in(key, 11))

    def shuffle(inner):
        return jax.random.permutation(inner, E_DEV)
    order = jax.vmap(shuffle)(jax.random.split(key_row, groups)).astype(jnp.int32)
    upward = jax.vmap(shuffle)(jax.random.split(key_col, groups)).astype(jnp.int32)
    lines = jnp.arange(groups, dtype=jnp.int32)[:, None]
    blank = jnp.zeros((groups, E_DEV), jnp.int32)
    east = blank.at[lines, order].set(jnp.roll(order, -1, axis=1)) + lines * E_DEV
    west = blank.at[lines, order].set(jnp.roll(order, 1, axis=1)) + lines * E_DEV
    north = upward + jnp.mod(lines + 1, groups) * E_DEV
    counter = jnp.broadcast_to(jnp.arange(E_DEV, dtype=jnp.int32)[None, :], (groups, E_DEV))
    below = blank.at[lines, upward].set(counter)
    south = jnp.roll(below, 1, axis=0) + jnp.mod(lines - 1, groups) * E_DEV
    return jnp.stack([west, east, south, north], axis=-1).reshape(ELEMS, 4).astype(jnp.int32)


def shard_levels(stream_key, dims, cuts, least, high):
    loudness = 1.0
    for position, parts in cuts:
        steps = jax.random.uniform(jax.random.fold_in(jax.random.fold_in(stream_key, 6), position), (parts,), jnp.float32, least / len(cuts), high / len(cuts))
        loudness = loudness * jnp.repeat(jnp.exp(steps), dims[position] // parts).reshape((-1,) + (1,) * (len(dims) - 1 - position))
    return loudness


def assign_block(rng, own, number, rows, number_of, top, most, lean):
    order = jax.random.permutation(rng, number_of)
    heavy_load, ordinary = portions_of(number_of, rows * top, most, lean, True), portions_of(number_of, rows * top, most, lean, False)
    places = jnp.arange(number_of)

    def named(sizes, offset_by):
        used = int((sizes > 0).sum())
        fixed = max(1, used // 4)
        passed = fixed + (places - fixed + offset_by * (used - fixed)) % max(1, number_of - fixed)
        return jnp.zeros((number_of,), jnp.int32).at[order[jnp.where(places < fixed, places, passed)]].set(jnp.asarray(sizes, jnp.int32))

    sizes = jnp.where(number % 4 == 0, named(heavy_load, number // 4), named(ordinary, number - number // 4 - 1))
    mixed = jax.random.permutation(jax.random.fold_in(own, 3), number_of)
    giver, receiver = mixed[0:number_of // 2 * 2:2], mixed[1:number_of // 2 * 2:2]
    room = jnp.minimum(sizes[giver] - 1, most - sizes[receiver]) // 2
    room = jnp.where((giver == order[0]) | (receiver == order[0]) | (sizes[receiver] == 0), 0, jnp.maximum(room, 0))
    passed = jax.random.randint(jax.random.fold_in(own, 4), (number_of // 2,), 0, 1 << 20) % (room + 1)
    sizes = sizes.at[giver].add(-passed).at[receiver].add(passed)
    members = jnp.searchsorted(jnp.cumsum(sizes), jnp.arange(rows * top), side="right").astype(jnp.int32)
    grid = members.reshape(top, rows).T
    grid = grid[jax.random.permutation(jax.random.fold_in(own, 1), rows)]
    offset_by = jax.random.randint(jax.random.fold_in(own, 2), (rows, 1), 0, top)
    return jnp.take_along_axis(grid, (jnp.arange(top)[None, :] + offset_by) % top, axis=1)


def portions_of(amount, total, reach, slope, full):
    weights = [(1 << 20) // math.isqrt(rank ** slope) + 1 for rank in range(1, amount + 1)]
    largest = reach if full else min(reach, max(-(-total // amount), total * weights[0] // sum(weights)))
    least = 1 if total - largest >= amount - 1 else 0
    given, spare = [largest] + [least] * (amount - 1), total - largest - least * (amount - 1)
    while spare > 0:
        movable = [i for i in range(1, amount) if given[i] < largest] or [i for i in range(1, amount) if given[i] < reach]
        mass, budget = sum([weights[i] for i in movable]), spare
        for i in movable:
            extra = min(reach - given[i], max(1, budget * weights[i] // mass), spare)
            given[i] = given[i] + extra
            spare = spare - extra
    return np.array(given)


def centred(key, dims, scale, bound, pieces=(), kind=jnp.bfloat16):
    loudness = shard_levels(key, dims, pieces, -0.22, 0.18) if pieces else 1.0
    values = jax.random.normal(key, dims, jnp.float32) * scale * loudness
    return jnp.minimum(jnp.maximum(values, -bound), bound).astype(kind)


def setup_inputs(seed: int = 0) -> dict:
    key_of = jax.random.split(jax.random.key(seed), 9)
    fields = centred(key_of[0], (ELEMS, POINTS, F), 1.0, 6.0, ((0, 256),), jnp.float32)
    neighbours = draw_neighbours(jax.random.fold_in(key_of[8], 71), 0)
    operator = centred(key_of[2], (POINTS, POINTS), POINTS ** -0.5, 1.5, (), jnp.float32)
    rates = jnp.clip(jnp.exp(jax.random.uniform(key_of[3], (F,), jnp.float32, math.log(0.05), math.log(0.5))), 0.05, 0.5)
    regime_ids_keys = jax.random.split(jax.random.fold_in(key_of[4], 1), COLS // COLS_DEV)
    regime_ids_turns = jax.random.permutation(jax.random.fold_in(key_of[4], 3), COLS // COLS_DEV)
    regime_ids = jax.vmap(lambda own, number: assign_block(jax.random.fold_in(key_of[4], 2), own, number, COLS_DEV, REGIMES, 1, CAP, 2))(regime_ids_keys, regime_ids_turns).reshape((COLS, 1))
    input_proj = centred(key_of[5], (REGIMES, F, HID), (F // 3) ** -0.5, 0.4375, ((0, 64), (2, 4)))
    hidden_proj = centred(key_of[6], (REGIMES, MID, HID, HID), (HID // 2) ** -0.5, 0.25, ((0, 64), (3, 4)))
    output_proj = centred(key_of[7], (REGIMES, HID, F), (HID // 2) ** -0.5, 0.25, ((0, 64), (2, 4)))
    return {"fields": fields, "neighbours": neighbours, "operator": operator, "rates": rates, "regime_ids": regime_ids, "input_proj": input_proj, "hidden_proj": hidden_proj, "output_proj": output_proj}


west_points = np.array([0, 4, 8, 12])
east_points = np.array([3, 7, 11, 15])
south_points = np.array([0, 1, 2, 3])
north_points = np.array([12, 13, 14, 15])


def dynamics(state, neighbours, operator, rates):
    moved = jnp.einsum("pq,eqf->epf", operator, state, precision=lax.Precision.HIGHEST)
    first = state + rates * moved
    left = first[:, west_points]
    right = first[:, east_points]
    new_left = 0.5 * (left + right[neighbours[:, 0]])
    new_right = 0.5 * (right + left[neighbours[:, 1]])
    second = first.at[:, west_points].set(new_left).at[:, east_points].set(new_right)
    lower = second[:, south_points]
    upper = second[:, north_points]
    new_lower = 0.5 * (lower + upper[neighbours[:, 2]])
    new_upper = 0.5 * (upper + lower[neighbours[:, 3]])
    return second.at[:, south_points].set(new_lower).at[:, north_points].set(new_upper)


def network_apply(rows, first_layer, middle, last_layer):
    hidden = jax.nn.silu(jnp.dot(rows, first_layer, preferred_element_type=jnp.float32)).astype(jnp.bfloat16)
    for layer in range(MID):
        hidden = jax.nn.silu(jnp.dot(hidden, middle[layer], preferred_element_type=jnp.float32)).astype(jnp.bfloat16)
    return jnp.dot(hidden, last_layer, preferred_element_type=jnp.float32).astype(jnp.bfloat16)


def reference(fields, neighbours, operator, rates, regime_ids, input_proj, hidden_proj, output_proj):
    state = fields
    for _ in range(DYN_STEPS):
        state = dynamics(state, neighbours, operator, rates)
    columns = state.reshape(COLS, F).astype(jnp.bfloat16)
    target = regime_ids[:, 0].reshape(DEVICES, COLS_DEV)
    onehot = (target[:, :, None] == jnp.arange(REGIMES, dtype=jnp.int32)[None, None, :]).astype(jnp.int32)
    ranking = jnp.sum((jnp.cumsum(onehot, axis=1) - 1) * onehot, axis=2)
    owner = jnp.arange(DEVICES, dtype=jnp.int32)[:, None]
    flat = (target * (DEVICES * CAP) + owner * CAP + ranking).reshape(COLS).astype(jnp.int32)
    buffer = jnp.zeros((REGIMES * DEVICES * CAP, F), jnp.bfloat16).at[flat].set(columns)
    grouped = buffer.reshape(REGIMES, DEVICES * CAP, F)

    def run_group(group):
        return network_apply(group[0], group[1], group[2], group[3])

    results = lax.map(run_group, (grouped, input_proj, hidden_proj, output_proj))
    tendency = results.reshape(REGIMES * DEVICES * CAP, F)[flat]
    return state + tendency.astype(jnp.float32).reshape(ELEMS, POINTS, F)
```

```python
import functools

import jax
import jax.numpy as jnp
from jax import lax
from jax.experimental import pallas as pl
from jax.experimental.pallas import tpu as pltpu
from jax.sharding import PartitionSpec as P

F32 = jnp.float32
BF16 = jnp.bfloat16
POINTS = 16
SIDE = 4
DEVICE_AXES = ("elem", "sec")
NT = (((1,), (1,)), ((), ()))
VMEM_LIMIT = 48 * 1024 * 1024


def iota(shape, axis):
    return lax.broadcasted_iota(jnp.int32, shape, axis)


def ones_where(mask):
    return jnp.where(mask, 1.0, 0.0).astype(BF16)


def mul(a, b):
    return jnp.dot(a, b, preferred_element_type=F32)


def mul_nt(a, b):
    return lax.dot_general(a, b, NT, preferred_element_type=F32)


def halves(x):
    high = x.astype(BF16)
    return high, (x - high.astype(F32)).astype(BF16)


def operator_blocks(op):
    size = POINTS * POINTS
    repeat = ones_where((iota((size, POINTS), 0) & (POINTS - 1)) == iota((size, POINTS), 1))
    same = (iota((size, size), 0) >> 4) == (iota((size, size), 1) >> 4)
    blocks = []
    for part in halves(op):
        tall = mul(repeat, part).astype(BF16)
        blocks.append(jnp.where(same, mul_nt(tall, repeat), 0.0).astype(BF16))
    return blocks


def neighbour_columns(nbt):
    count = nbt.shape[1]
    rows = count * POINTS
    spread = ones_where((iota((rows, count), 0) >> 4) == iota((rows, count), 1))
    local = (nbt & (count - 1)).astype(F32).astype(BF16)
    return mul_nt(spread, local)


def advance(state, op, rates, nbt):
    rows = state.shape[0]
    size = POINTS * POINTS
    op_high, op_low = operator_blocks(op)
    moved = []
    for start in range(0, rows, size):
        high, low = halves(state[start : start + size])
        moved.append(mul(op_high, high) + (mul(op_high, low) + mul(op_low, high)))
    first = state + rates * jnp.concatenate(moved, axis=0)
    near = neighbour_columns(nbt)
    place = iota((rows, 1), 0) & (POINTS - 1)
    column = place & (SIDE - 1)
    west = column == 0
    east = column == SIDE - 1
    placef = place.astype(F32)
    source = jnp.where(
        west,
        near[:, 0:1] * POINTS + placef + (SIDE - 1),
        jnp.where(east, near[:, 1:2] * POINTS + placef - (SIDE - 1), -1.0),
    )
    pick = ones_where(iota((rows, rows), 1).astype(F32) == source)
    high, low = halves(first)
    far = mul(pick, high) + mul(pick, low)
    return jnp.where(west | east, 0.5 * (first + far), first)


def edges(second):
    rows = second.shape[0]
    count = rows // POINTS * SIDE
    j = iota((2 * count, 1), 0)
    k = j & (count - 1)
    source = (k >> 2) * POINTS + (k & (SIDE - 1)) + jnp.where(j < count, POINTS - SIDE, 0)
    pick = ones_where(iota((2 * count, rows), 1) == source)
    return mul(pick, second.astype(BF16)).astype(BF16)


def meet(second, below, above, nbt):
    rows = second.shape[0]
    count = below.shape[0]
    near = neighbour_columns(nbt)
    place = iota((rows, 1), 0) & (POINTS - 1)
    south = place < SIDE
    north = place >= POINTS - SIDE
    placef = place.astype(F32)
    source = jnp.where(
        south,
        near[:, 2:3] * SIDE + placef,
        jnp.where(north, near[:, 3:4] * SIDE + placef + (count - (POINTS - SIDE)), -1.0),
    )
    pick = ones_where(iota((rows, 2 * count), 1).astype(F32) == source)
    far = mul(pick, jnp.concatenate([below, above], axis=0))
    return jnp.where(south | north, 0.5 * (second + far), second)


def start_kernel(state_ref, nbt_ref, op_ref, rates_ref, second_ref, north_ref, south_ref):
    second = advance(state_ref[...], op_ref[...], rates_ref[...], nbt_ref[...])
    second_ref[...] = second
    sides = edges(second)
    count = north_ref.shape[0]
    north_ref[...] = sides[:count]
    south_ref[...] = sides[count:]


def step_kernel(
    prev_ref, below_ref, above_ref, nbt_ref, op_ref, rates_ref, second_ref, north_ref, south_ref
):
    nbt = nbt_ref[...]
    state = meet(prev_ref[...], below_ref[...], above_ref[...], nbt)
    second = advance(state, op_ref[...], rates_ref[...], nbt)
    second_ref[...] = second
    sides = edges(second)
    count = north_ref.shape[0]
    north_ref[...] = sides[:count]
    south_ref[...] = sides[count:]


def send_kernel(capacity, groups, prev_ref, below_ref, above_ref, nbt_ref, ids_ref, state_ref, out_ref):
    state = meet(prev_ref[...], below_ref[...], above_ref[...], nbt_ref[...])
    state_ref[...] = state
    rows = state.shape[0]
    named = iota((groups, rows), 0) == ids_ref[...]
    upto = ones_where(iota((rows, rows), 0) <= iota((rows, rows), 1))
    rank = mul(ones_where(named), upto)
    base = (iota((groups, rows), 0) * capacity - 1).astype(F32)
    slot = jnp.sum(jnp.where(named, base + rank, 0.0), axis=0, keepdims=True)
    pick = ones_where(iota((groups * capacity, rows), 0).astype(F32) == slot)
    out_ref[...] = mul(pick, state.astype(BF16)).astype(BF16)


def add_kernel(capacity, groups, state_ref, back_ref, ids_ref, out_ref):
    rows = state_ref.shape[0]
    same = ones_where(iota((rows, rows), 0) == iota((rows, rows), 1))
    ids = jnp.broadcast_to(ids_ref[...].astype(F32).astype(BF16), (8, rows))
    regime = mul_nt(same, ids)[:, 0:1]
    lanes = iota((rows, groups), 1)
    named = lanes.astype(F32) == regime
    upto = ones_where(iota((rows, rows), 1) <= iota((rows, rows), 0))
    rank = mul(upto, ones_where(named))
    base = (lanes * capacity - 1).astype(F32)
    slot = jnp.sum(jnp.where(named, base + rank, 0.0), axis=1, keepdims=True)
    pick = ones_where(iota((rows, groups * capacity), 1).astype(F32) == slot)
    out_ref[...] = state_ref[...] + mul(pick, back_ref[...])


def silu(v):
    half = 0.5 * v
    return (half + half * jnp.tanh(half)).astype(BF16)


def network_kernel(tile, sec_ref, rows_ref, *refs):
    first, middle, last = refs[0:4], refs[4:8], refs[8:12]
    out_ref, hold_a, hold_b, last_all = refs[12:]
    places = [(sec_ref[0] + k) & 3 for k in range(4)]
    width = first[0].shape[1]
    for k in range(4):
        last_all[places[k]] = last[k][...]

    def body(step, carry):
        at = pl.ds(pl.multiple_of(step * tile, tile), tile)
        rows = rows_ref[at, :]
        for k in range(4):
            spot = pl.ds(pl.multiple_of(places[k] * width, width), width)
            hold_a[:, spot] = silu(mul(rows, first[k][...]))
        now, later = hold_a, hold_b
        for layer in range(middle[0].shape[0]):
            for k in range(4):
                spot = pl.ds(pl.multiple_of(places[k] * width, width), width)
                later[:, spot] = silu(mul(now[...], middle[k][layer]))
            now, later = later, now
        matrix = last_all[...].reshape(out_ref.shape[1], now.shape[1])
        out_ref[at, :] = mul_nt(now[...], matrix).astype(BF16)
        return carry

    lax.fori_loop(0, rows_ref.shape[0] // tile, body, 0)


def call(kernel, out, *args, scratch=(), flops=0, specs=None):
    size = sum(a.size * a.dtype.itemsize for a in args)
    size += sum(o.size * o.dtype.itemsize for o in out)
    vmem = pl.BlockSpec(memory_space=pltpu.VMEM)
    return pl.pallas_call(
        kernel,
        out_shape=out,
        in_specs=specs or [vmem] * len(args),
        out_specs=[vmem] * len(out),
        scratch_shapes=scratch,
        compiler_params=pltpu.CompilerParams(vmem_limit_bytes=VMEM_LIMIT),
        cost_estimate=pl.CostEstimate(flops=flops, bytes_accessed=size, transcendentals=0),
    )(*args)


def ring(count, step):
    return [(i, (i + step) % count) for i in range(count)]


def exchange(north, south):
    total = lax.axis_size(DEVICE_AXES)
    below = lax.ppermute(north, DEVICE_AXES, ring(total, 1))
    above = lax.ppermute(south, DEVICE_AXES, ring(total, -1))
    return below, above


def gathered(shard):
    return [shard] + [lax.ppermute(shard, "sec", ring(4, -k)) for k in (1, 2, 3)]


def on_device(
    fields, neighbours, operator, rates, regime_ids, input_proj, hidden_proj, output_proj
):
    count, points, width = fields.shape
    rows_dev = count * points
    groups = lax.axis_size("elem")
    capacity = 2 * rows_dev // groups
    slots = groups * capacity
    shape = jax.ShapeDtypeStruct
    nbt = neighbours.T
    ids = regime_ids.T
    rate_row = rates.reshape(1, width)

    first = gathered(input_proj[0])
    middle = gathered(hidden_proj[0])
    last = gathered(output_proj[0].T)

    edge = shape((count * SIDE, width), BF16)
    moved = [shape((rows_dev, width), F32), edge, edge]
    second, north, south = call(
        start_kernel, moved, fields.reshape(rows_dev, width), nbt, operator, rate_row, flops=3 * 10**9
    )
    below, above = exchange(north, south)
    second, north, south = call(
        step_kernel, moved, second, below, above, nbt, operator, rate_row, flops=3 * 10**9
    )
    below, above = exchange(north, south)
    state, outgoing = call(
        functools.partial(send_kernel, capacity, groups),
        [shape((rows_dev, width), F32), shape((slots, width), BF16)],
        second, below, above, nbt, ids, flops=3 * 10**9,
    )
    incoming = lax.all_to_all(
        outgoing.reshape(groups, capacity, width), "elem", split_axis=0, concat_axis=0, tiled=True
    )
    hid = hidden_proj.shape[2]
    tile = 512
    vmem = pl.BlockSpec(memory_space=pltpu.VMEM)
    sec = lax.axis_index("sec").astype(jnp.int32).reshape(1)
    (result,) = call(
        functools.partial(network_kernel, tile),
        [shape((slots, width), BF16)],
        sec, incoming.reshape(slots, width), *first, *middle, *last,
        scratch=[
            pltpu.VMEM((tile, hid), BF16),
            pltpu.VMEM((tile, hid), BF16),
            pltpu.VMEM((4, width // 4, hid), BF16),
        ],
        specs=[pl.BlockSpec(memory_space=pltpu.SMEM)] + [vmem] * 13,
        flops=7 * 10**9,
    )
    returned = lax.all_to_all(
        result.reshape(groups, capacity, width), "elem", split_axis=0, concat_axis=0, tiled=True
    )
    (updated,) = call(
        functools.partial(add_kernel, capacity, groups),
        [shape((rows_dev, width), F32)],
        state, returned.reshape(slots, width), ids, flops=10**9,
    )
    return updated.reshape(count, points, width)


def solution(mesh):
    return jax.shard_map(
        on_device,
        mesh=mesh,
        in_specs=(
            P(DEVICE_AXES, None, None),
            P(DEVICE_AXES, None),
            P(),
            P(),
            P(DEVICE_AXES, None),
            P("elem", None, "sec"),
            P("elem", None, None, "sec"),
            P("elem", None, "sec"),
        ),
        out_specs=P(DEVICE_AXES, None, None),
        check_vma=False,
    )
```

```python
import functools

import jax
import jax.numpy as jnp
from jax import lax
from jax.experimental import pallas as pl
from jax.experimental.pallas import tpu as pltpu
from jax.sharding import PartitionSpec as P

F32 = jnp.float32
BF16 = jnp.bfloat16
POINTS = 16
SIDE = 4
DEVICE_AXES = ("elem", "sec")
NT = (((1,), (1,)), ((), ()))
VMEM_LIMIT = 40 * 1024 * 1024


def iota(shape, axis):
    return lax.broadcasted_iota(jnp.int32, shape, axis)


def ones_where(mask):
    return jnp.where(mask, 1.0, 0.0).astype(BF16)


def mul(a, b):
    return jnp.dot(a, b, preferred_element_type=F32)


def mul_nt(a, b):
    return lax.dot_general(a, b, NT, preferred_element_type=F32)


def halves(x):
    high = x.astype(BF16)
    return high, (x - high.astype(F32)).astype(BF16)


def operator_blocks(op):
    size = POINTS * POINTS
    repeat = ones_where((iota((size, POINTS), 0) & (POINTS - 1)) == iota((size, POINTS), 1))
    same = (iota((size, size), 0) >> 4) == (iota((size, size), 1) >> 4)
    blocks = []
    for part in halves(op):
        tall = mul(repeat, part).astype(BF16)
        blocks.append(jnp.where(same, mul_nt(tall, repeat), 0.0).astype(BF16))
    return blocks


def neighbour_columns(nbt):
    count = nbt.shape[1]
    rows = count * POINTS
    spread = ones_where((iota((rows, count), 0) >> 4) == iota((rows, count), 1))
    local = (nbt & (count - 1)).astype(F32).astype(BF16)
    return mul_nt(spread, local)


def advance(state, op, rates, nbt):
    rows = state.shape[0]
    size = POINTS * POINTS
    op_high, op_low = operator_blocks(op)
    moved = []
    for start in range(0, rows, size):
        high, low = halves(state[start : start + size])
        moved.append(mul(op_high, high) + (mul(op_high, low) + mul(op_low, high)))
    first = state + rates * jnp.concatenate(moved, axis=0)
    near = neighbour_columns(nbt)
    place = iota((rows, 1), 0) & (POINTS - 1)
    column = place & (SIDE - 1)
    west = column == 0
    east = column == SIDE - 1
    placef = place.astype(F32)
    source = jnp.where(
        west,
        near[:, 0:1] * POINTS + placef + (SIDE - 1),
        jnp.where(east, near[:, 1:2] * POINTS + placef - (SIDE - 1), -1.0),
    )
    pick = ones_where(iota((rows, rows), 1).astype(F32) == source)
    high, low = halves(first)
    far = mul(pick, high) + mul(pick, low)
    return jnp.where(west | east, 0.5 * (first + far), first)


def edges(second):
    rows = second.shape[0]
    count = rows // POINTS * SIDE
    j = iota((2 * count, 1), 0)
    k = j & (count - 1)
    source = (k >> 2) * POINTS + (k & (SIDE - 1)) + jnp.where(j < count, POINTS - SIDE, 0)
    pick = ones_where(iota((2 * count, rows), 1) == source)
    return mul(pick, second.astype(BF16)).astype(BF16)


def meet(second, below, above, nbt):
    rows = second.shape[0]
    count = below.shape[0]
    near = neighbour_columns(nbt)
    place = iota((rows, 1), 0) & (POINTS - 1)
    south = place < SIDE
    north = place >= POINTS - SIDE
    placef = place.astype(F32)
    source = jnp.where(
        south,
        near[:, 2:3] * SIDE + placef,
        jnp.where(north, near[:, 3:4] * SIDE + placef + (count - (POINTS - SIDE)), -1.0),
    )
    pick = ones_where(iota((rows, 2 * count), 1).astype(F32) == source)
    far = mul(pick, jnp.concatenate([below, above], axis=0))
    return jnp.where(south | north, 0.5 * (second + far), second)


def start_kernel(
    state_ref, nbt_ref, op_ref, rates_ref, second_ref, north_ref, south_ref, state, nbt, op, rates, sems
):
    pairs = [(state_ref, state), (nbt_ref, nbt), (op_ref, op), (rates_ref, rates)]
    copies = [pltpu.make_async_copy(a, b, sems.at[i]) for i, (a, b) in enumerate(pairs)]
    for copy in copies:
        copy.start()
    for copy in copies:
        copy.wait()
    second = advance(state[...], op[...], rates[...].reshape(1, -1), nbt[...])
    second_ref[...] = second
    sides = edges(second)
    count = north_ref.shape[0]
    north_ref[...] = sides[:count]
    south_ref[...] = sides[count:]


def step_kernel(
    prev_ref, below_ref, above_ref, nbt_ref, op_ref, rates_ref, *refs
):
    second_ref, north_ref, south_ref = refs[-3:]
    nbt = nbt_ref[...]
    state = meet(prev_ref[...], below_ref[...], above_ref[...], nbt)
    second = advance(state, op_ref[...], rates_ref[...].reshape(1, -1), nbt)
    second_ref[...] = second
    sides = edges(second)
    count = north_ref.shape[0]
    north_ref[...] = sides[:count]
    south_ref[...] = sides[count:]


def send_kernel(capacity, groups, prev_ref, below_ref, above_ref, nbt_ref, ids_ref, *refs):
    state_ref, out_ref = refs[-2:]
    state = meet(prev_ref[...], below_ref[...], above_ref[...], nbt_ref[...])
    state_ref[...] = state
    rows = state.shape[0]
    named = iota((groups, rows), 0) == ids_ref[...]
    upto = ones_where(iota((rows, rows), 0) <= iota((rows, rows), 1))
    rank = mul(ones_where(named), upto)
    base = (iota((groups, rows), 0) * capacity - 1).astype(F32)
    slot = jnp.sum(jnp.where(named, base + rank, 0.0), axis=0, keepdims=True)
    pick = ones_where(iota((groups * capacity, rows), 0).astype(F32) == slot)
    out_ref[...] = mul(pick, state.astype(BF16)).astype(BF16)


def add_kernel(capacity, groups, state_ref, back_ref, ids_ref, out_ref):
    rows = state_ref.shape[0]
    same = ones_where(iota((rows, rows), 0) == iota((rows, rows), 1))
    ids = jnp.broadcast_to(ids_ref[...].astype(F32).astype(BF16), (8, rows))
    regime = mul_nt(same, ids)[:, 0:1]
    lanes = iota((rows, groups), 1)
    named = lanes.astype(F32) == regime
    upto = ones_where(iota((rows, rows), 1) <= iota((rows, rows), 0))
    rank = mul(upto, ones_where(named))
    base = (lanes * capacity - 1).astype(F32)
    slot = jnp.sum(jnp.where(named, base + rank, 0.0), axis=1, keepdims=True)
    pick = ones_where(iota((rows, groups * capacity), 1).astype(F32) == slot)
    out_ref[...] = state_ref[...] + mul(pick, back_ref[...])


def silu(v):
    half = 0.5 * v
    return (half + half * jnp.tanh(half)).astype(BF16)


def network_kernel(tile, sec_ref, rows_ref, *refs):
    shards, out_ref = refs[0:12], refs[12]
    first, middle, last, hold_a, hold_b, sems = refs[13:]
    layers = middle.shape[1]
    places = [(sec_ref[0] + k) & 3 for k in range(4)]
    width = first.shape[2]
    waits = [[] for _ in range(layers + 2)]
    for k in range(4):
        pairs = [(shards[k], first.at[k], 0)]
        pairs += [(shards[4 + k].at[layer], middle.at[k, layer], 1 + layer) for layer in range(layers)]
        pairs += [(shards[8 + k], last.at[places[k]], 1 + layers)]
        for source, target, group in pairs:
            waits[group].append(pltpu.make_async_copy(source, target, sems.at[k, group]))
    for group in waits:
        for copy in group:
            copy.start()

    def arrived(start, group):
        if start == 0:
            for copy in waits[group]:
                copy.wait()

    for start in range(0, rows_ref.shape[0], tile):
        rows = rows_ref[start : start + tile]
        arrived(start, 0)
        for k in range(4):
            spot = pl.ds(pl.multiple_of(places[k] * width, width), width)
            hold_a[:, spot] = silu(mul(rows, first[k]))
        now, later = hold_a, hold_b
        for layer in range(layers):
            arrived(start, 1 + layer)
            for k in range(4):
                spot = pl.ds(pl.multiple_of(places[k] * width, width), width)
                later[:, spot] = silu(mul(now[...], middle[k, layer]))
            now, later = later, now
        arrived(start, 1 + layers)
        matrix = last[...].reshape(out_ref.shape[1], now.shape[1])
        out_ref[start : start + tile] = mul_nt(now[...], matrix).astype(BF16)


def call(kernel, out, *args, passed=(), scratch=(), flops=0, specs=None, limit=VMEM_LIMIT):
    size = sum(a.size * a.dtype.itemsize for a in args)
    size += sum(o.size * o.dtype.itemsize for o in out)
    vmem = pl.BlockSpec(memory_space=pltpu.VMEM)
    return pl.pallas_call(
        kernel,
        out_shape=out,
        in_specs=(specs or [vmem] * len(args)) + [pl.BlockSpec(memory_space=pl.ANY)] * len(passed),
        out_specs=[vmem] * len(out),
        scratch_shapes=scratch,
        compiler_params=pltpu.CompilerParams(vmem_limit_bytes=limit),
        cost_estimate=pl.CostEstimate(flops=flops, bytes_accessed=size, transcendentals=0),
    )(*args, *passed)


def ring(count, step):
    return [(i, (i + step) % count) for i in range(count)]


def exchange(north, south):
    total = lax.axis_size(DEVICE_AXES)
    below = lax.ppermute(north, DEVICE_AXES, ring(total, 1))
    above = lax.ppermute(south, DEVICE_AXES, ring(total, -1))
    return below, above


def gathered(shard):
    return [shard] + [lax.ppermute(shard, "sec", ring(4, -k)) for k in (1, 2, 3)]


def on_device(
    fields, neighbours, operator, rates, regime_ids, input_proj, hidden_proj, output_proj
):
    count, points, width = fields.shape
    rows_dev = count * points
    groups = lax.axis_size("elem")
    capacity = 2 * rows_dev // groups
    slots = groups * capacity
    shape = jax.ShapeDtypeStruct
    nbt = neighbours.T
    ids = regime_ids.T

    first = gathered(input_proj[0])
    middle = gathered(hidden_proj[0])
    last = gathered(output_proj[0].T)

    edge = shape((count * SIDE, width), BF16)
    moved = [shape((rows_dev, width), F32), edge, edge]
    second, north, south = call(
        start_kernel, moved, fields.reshape(rows_dev, width), nbt, operator, rates,
        scratch=[
            pltpu.VMEM((rows_dev, width), F32),
            pltpu.VMEM(nbt.shape, jnp.int32),
            pltpu.VMEM(operator.shape, F32),
            pltpu.VMEM(rates.shape, F32),
            pltpu.SemaphoreType.DMA((4,)),
        ],
        specs=[pl.BlockSpec(memory_space=pl.ANY)] * 4,
        limit=58 * 1024 * 1024,
        flops=3 * 10**9,
    )
    below, above = exchange(north, south)
    second, north, south = call(
        step_kernel, moved, second, below, above, nbt, operator, rates, passed=first[1:], flops=3 * 10**9
    )
    below, above = exchange(north, south)
    state, outgoing = call(
        functools.partial(send_kernel, capacity, groups),
        [shape((rows_dev, width), F32), shape((slots, width), BF16)],
        second, below, above, nbt, ids, passed=last[1:], flops=3 * 10**9,
    )
    incoming = lax.all_to_all(
        outgoing.reshape(groups, capacity, width), "elem", split_axis=0, concat_axis=0, tiled=True
    )
    hid = hidden_proj.shape[2]
    tile = 512
    vmem = pl.BlockSpec(memory_space=pltpu.VMEM)
    sec = lax.axis_index("sec").astype(jnp.int32).reshape(1)
    (result,) = call(
        functools.partial(network_kernel, tile),
        [shape((slots, width), BF16)],
        sec, incoming.reshape(slots, width), *first, *middle, *last,
        scratch=[
            pltpu.VMEM((4, *input_proj.shape[1:2], hid // 4), BF16),
            pltpu.VMEM((4, *hidden_proj.shape[1:3], hid // 4), BF16),
            pltpu.VMEM((4, width // 4, hid), BF16),
            pltpu.VMEM((tile, hid), BF16),
            pltpu.VMEM((tile, hid), BF16),
            pltpu.SemaphoreType.DMA((4, 2 + hidden_proj.shape[1])),
        ],
        specs=[pl.BlockSpec(memory_space=pltpu.SMEM), vmem] + [pl.BlockSpec(memory_space=pl.ANY)] * 12,
        limit=55 * 1024 * 1024,
        flops=7 * 10**9,
    )
    returned = lax.all_to_all(
        result.reshape(groups, capacity, width), "elem", split_axis=0, concat_axis=0, tiled=True
    )
    (updated,) = call(
        functools.partial(add_kernel, capacity, groups),
        [shape((rows_dev, width), F32)],
        state, returned.reshape(slots, width), ids, flops=10**9,
    )
    return updated.reshape(count, points, width)


def solution(mesh):
    return jax.shard_map(
        on_device,
        mesh=mesh,
        in_specs=(
            P(DEVICE_AXES, None, None),
            P(DEVICE_AXES, None),
            P(),
            P(),
            P(DEVICE_AXES, None),
            P("elem", None, "sec"),
            P("elem", None, None, "sec"),
            P("elem", None, "sec"),
        ),
        out_specs=P(DEVICE_AXES, None, None),
        check_vma=False,
    )
```

```python
import functools

import jax
import jax.numpy as jnp
from jax import lax
from jax.experimental import pallas as pl
from jax.experimental.pallas import tpu as pltpu
from jax.sharding import PartitionSpec as P

F32 = jnp.float32
BF16 = jnp.bfloat16
POINTS = 16
SIDE = 4
DEVICE_AXES = ("elem", "sec")
NT = (((1,), (1,)), ((), ()))
VMEM_LIMIT = 40 * 1024 * 1024


def iota(shape, axis):
    return lax.broadcasted_iota(jnp.int32, shape, axis)


def ones_where(mask):
    return jnp.where(mask, 1.0, 0.0).astype(BF16)


def mul(a, b):
    return jnp.dot(a, b, preferred_element_type=F32)


def mul_nt(a, b):
    return lax.dot_general(a, b, NT, preferred_element_type=F32)


def halves(x):
    high = x.astype(BF16)
    return high, (x - high.astype(F32)).astype(BF16)


def operator_blocks(op):
    size = POINTS * POINTS
    repeat = ones_where((iota((size, POINTS), 0) & (POINTS - 1)) == iota((size, POINTS), 1))
    same = (iota((size, size), 0) >> 4) == (iota((size, size), 1) >> 4)
    blocks = []
    for part in halves(op):
        tall = mul(repeat, part).astype(BF16)
        blocks.append(jnp.where(same, mul_nt(tall, repeat), 0.0).astype(BF16))
    return blocks


def neighbour_columns(nbt):
    count = nbt.shape[1]
    rows = count * POINTS
    spread = ones_where((iota((rows, count), 0) >> 4) == iota((rows, count), 1))
    local = (nbt & (count - 1)).astype(F32).astype(BF16)
    return mul_nt(spread, local)


def advance(state, op, rates, nbt):
    rows = state.shape[0]
    size = POINTS * POINTS
    op_high, op_low = operator_blocks(op)
    moved = []
    for start in range(0, rows, size):
        high, low = halves(state[start : start + size])
        moved.append(mul(op_high, high) + (mul(op_high, low) + mul(op_low, high)))
    first = state + rates * jnp.concatenate(moved, axis=0)
    near = neighbour_columns(nbt)
    place = iota((rows, 1), 0) & (POINTS - 1)
    column = place & (SIDE - 1)
    west = column == 0
    east = column == SIDE - 1
    placef = place.astype(F32)
    source = jnp.where(
        west,
        near[:, 0:1] * POINTS + placef + (SIDE - 1),
        jnp.where(east, near[:, 1:2] * POINTS + placef - (SIDE - 1), -1.0),
    )
    pick = ones_where(iota((rows, rows), 1).astype(F32) == source)
    high, low = halves(first)
    far = mul(pick, high) + mul(pick, low)
    return jnp.where(west | east, 0.5 * (first + far), first)


def edges(second):
    rows = second.shape[0]
    count = rows // POINTS * SIDE
    j = iota((2 * count, 1), 0)
    k = j & (count - 1)
    source = (k >> 2) * POINTS + (k & (SIDE - 1)) + jnp.where(j < count, POINTS - SIDE, 0)
    pick = ones_where(iota((2 * count, rows), 1) == source)
    return mul(pick, second.astype(BF16)).astype(BF16)


def meet(second, below, above, nbt):
    rows = second.shape[0]
    count = below.shape[0]
    near = neighbour_columns(nbt)
    place = iota((rows, 1), 0) & (POINTS - 1)
    south = place < SIDE
    north = place >= POINTS - SIDE
    placef = place.astype(F32)
    source = jnp.where(
        south,
        near[:, 2:3] * SIDE + placef,
        jnp.where(north, near[:, 3:4] * SIDE + placef + (count - (POINTS - SIDE)), -1.0),
    )
    pick = ones_where(iota((rows, 2 * count), 1).astype(F32) == source)
    far = mul(pick, jnp.concatenate([below, above], axis=0))
    return jnp.where(south | north, 0.5 * (second + far), second)


def start_kernel(
    state_ref, nbt_ref, op_ref, rates_ref, second_ref, north_ref, south_ref, state, nbt, op, rates, sems
):
    pairs = [(state_ref, state), (nbt_ref, nbt), (op_ref, op), (rates_ref, rates)]
    copies = [pltpu.make_async_copy(a, b, sems.at[i]) for i, (a, b) in enumerate(pairs)]
    for copy in copies:
        copy.start()
    for copy in copies:
        copy.wait()
    second = advance(state[...], op[...], rates[...].reshape(1, -1), nbt[...])
    second_ref[...] = second
    sides = edges(second)
    count = north_ref.shape[0]
    north_ref[...] = sides[:count]
    south_ref[...] = sides[count:]


def step_kernel(
    prev_ref, below_ref, above_ref, nbt_ref, op_ref, rates_ref, *refs
):
    second_ref, north_ref, south_ref = refs[-3:]
    nbt = nbt_ref[...]
    state = meet(prev_ref[...], below_ref[...], above_ref[...], nbt)
    second = advance(state, op_ref[...], rates_ref[...].reshape(1, -1), nbt)
    second_ref[...] = second
    sides = edges(second)
    count = north_ref.shape[0]
    north_ref[...] = sides[:count]
    south_ref[...] = sides[count:]


def send_kernel(
    capacity, groups, prev_ref, below_ref, above_ref, nbt_ref, ids_ref, hidden_ref, *refs
):
    state_ref, out_ref, copy_ref, sem = refs[-4:]
    hand_on = pltpu.make_async_copy(hidden_ref, copy_ref, sem.at[0])
    hand_on.start()
    state = meet(prev_ref[...], below_ref[...], above_ref[...], nbt_ref[...])
    state_ref[...] = state
    rows = state.shape[0]
    named = iota((groups, rows), 0) == ids_ref[...]
    upto = ones_where(iota((rows, rows), 0) <= iota((rows, rows), 1))
    rank = mul(ones_where(named), upto)
    base = (iota((groups, rows), 0) * capacity - 1).astype(F32)
    slot = jnp.sum(jnp.where(named, base + rank, 0.0), axis=0, keepdims=True)
    pick = ones_where(iota((groups * capacity, rows), 0).astype(F32) == slot)
    out_ref[...] = mul(pick, state.astype(BF16)).astype(BF16)
    hand_on.wait()


def add_kernel(capacity, groups, state_ref, back_ref, ids_ref, out_ref):
    rows = state_ref.shape[0]
    same = ones_where(iota((rows, rows), 0) == iota((rows, rows), 1))
    ids = jnp.broadcast_to(ids_ref[...].astype(F32).astype(BF16), (8, rows))
    regime = mul_nt(same, ids)[:, 0:1]
    lanes = iota((rows, groups), 1)
    named = lanes.astype(F32) == regime
    upto = ones_where(iota((rows, rows), 1) <= iota((rows, rows), 0))
    rank = mul(upto, ones_where(named))
    base = (lanes * capacity - 1).astype(F32)
    slot = jnp.sum(jnp.where(named, base + rank, 0.0), axis=1, keepdims=True)
    pick = ones_where(iota((rows, groups * capacity), 1).astype(F32) == slot)
    out_ref[...] = state_ref[...] + mul(pick, back_ref[...])


def halves_kernel(below_ref, above_ref, low_ref, high_ref):
    low_ref[...] = below_ref[0]
    high_ref[...] = above_ref[1]


def silu(v):
    half = 0.5 * v
    return (half + half * jnp.tanh(half)).astype(BF16)


def network_kernel(tile, sec_ref, rows_ref, *refs):
    first_in, hidden_in, last_in, out_ref = refs[0:4], refs[4:9], refs[9:13], refs[13]
    first, middle, last, hold_a, hold_b, rows, result, sems, row_sems, out_sems = refs[14:]
    layers = middle.shape[1]
    tiles = rows.shape[0]
    places = [(sec_ref[0] + k) & 3 for k in range(4)]
    width = first.shape[2]
    at = [pl.ds(step * tile, tile) for step in range(tiles)]
    incoming = [pltpu.make_async_copy(rows_ref.at[at[i]], rows.at[i], row_sems.at[i]) for i in range(tiles)]
    outgoing = [pltpu.make_async_copy(result.at[i], out_ref.at[at[i]], out_sems.at[i]) for i in range(tiles)]
    weights = [[] for _ in range(layers + 2)]
    for k in range(4):
        pairs = [(first_in[k], first.at[k], 0)]
        for layer in range(layers):
            source = hidden_in[2 + layer] if k == 2 else hidden_in[(0, 1, 2, 4)[k]].at[layer]
            pairs += [(source, middle.at[k, layer], 1 + layer)]
        pairs += [(last_in[k], last.at[places[k]], 1 + layers)]
        for source, target, group in pairs:
            weights[group].append(pltpu.make_async_copy(source, target, sems.at[k, group]))
    incoming[0].start()
    for copy in weights[0]:
        copy.start()
    for step in range(tiles):
        incoming[step].wait()
        if step == 0:
            for copy in weights[0]:
                copy.wait()
            for group in weights[1:]:
                for copy in group:
                    copy.start()
            for copy in incoming[1:]:
                copy.start()
        for k in range(4):
            spot = pl.ds(pl.multiple_of(places[k] * width, width), width)
            hold_a[:, spot] = silu(mul(rows[step], first[k]))
        now, later = hold_a, hold_b
        for layer in range(layers):
            if step == 0:
                for copy in weights[1 + layer]:
                    copy.wait()
            for k in range(4):
                spot = pl.ds(pl.multiple_of(places[k] * width, width), width)
                later[:, spot] = silu(mul(now[...], middle[k, layer]))
            now, later = later, now
        if step == 0:
            for copy in weights[1 + layers]:
                copy.wait()
        matrix = last[...].reshape(out_ref.shape[1], now.shape[1])
        result[step] = mul_nt(now[...], matrix).astype(BF16)
        outgoing[step].start()
    for copy in outgoing:
        copy.wait()


def call(kernel, out, *args, passed=(), scratch=(), flops=0, specs=None, outs=None, limit=VMEM_LIMIT):
    size = sum(a.size * a.dtype.itemsize for a in args)
    size += sum(o.size * o.dtype.itemsize for o in out)
    vmem = pl.BlockSpec(memory_space=pltpu.VMEM)
    return pl.pallas_call(
        kernel,
        out_shape=out,
        in_specs=(specs or [vmem] * len(args)) + [pl.BlockSpec(memory_space=pl.ANY)] * len(passed),
        out_specs=outs or [vmem] * len(out),
        scratch_shapes=scratch,
        compiler_params=pltpu.CompilerParams(vmem_limit_bytes=limit),
        cost_estimate=pl.CostEstimate(flops=flops, bytes_accessed=size, transcendentals=0),
    )(*args, *passed)


def ring(count, step):
    return [(i, (i + step) % count) for i in range(count)]


def exchange(north, south):
    total = lax.axis_size(DEVICE_AXES)
    below = lax.ppermute(north, DEVICE_AXES, ring(total, 1))
    above = lax.ppermute(south, DEVICE_AXES, ring(total, -1))
    return below, above


def from_sides(*shards):
    below = [lax.ppermute(x, "sec", ring(4, 1)) for x in shards]
    above = [lax.ppermute(x, "sec", ring(4, -1)) for x in shards]
    return below, above


def from_far(below, above):
    return lax.ppermute(below, "sec", ring(4, 1)), lax.ppermute(above, "sec", ring(4, -1))


def on_device(
    fields, neighbours, operator, rates, regime_ids, input_proj, hidden_proj, output_proj
):
    count, points, width = fields.shape
    rows_dev = count * points
    groups = lax.axis_size("elem")
    capacity = 2 * rows_dev // groups
    slots = groups * capacity
    shape = jax.ShapeDtypeStruct
    nbt = neighbours.T
    ids = regime_ids.T

    mine = (input_proj[0], output_proj[0].T)
    below, above = from_sides(*mine)
    first, last = ([m, a, None, b] for m, a, b in zip(mine, above, below))
    first[2], last[2] = from_far(below[0], above[1])
    anywhere = pl.BlockSpec(memory_space=pl.ANY)

    edge = shape((count * SIDE, width), BF16)
    moved = [shape((rows_dev, width), F32), edge, edge]
    second, north, south = call(
        start_kernel, moved, fields.reshape(rows_dev, width), nbt, operator, rates,
        scratch=[
            pltpu.VMEM((rows_dev, width), F32),
            pltpu.VMEM(nbt.shape, jnp.int32),
            pltpu.VMEM(operator.shape, F32),
            pltpu.VMEM(rates.shape, F32),
            pltpu.SemaphoreType.DMA((4,)),
        ],
        specs=[anywhere] * 4,
        limit=58 * 1024 * 1024,
        flops=3 * 10**9,
    )
    prev, next_ = exchange(north, south)
    vmem = pl.BlockSpec(memory_space=pltpu.VMEM)
    second, north, south = call(
        step_kernel, moved, second, prev, next_, nbt, operator, rates,
        passed=(below[0], above[0]), flops=3 * 10**9,
    )
    prev, next_ = exchange(north, south)
    state, outgoing, hidden_copy = call(
        functools.partial(send_kernel, capacity, groups),
        [
            shape((rows_dev, width), F32),
            shape((slots, width), BF16),
            shape(hidden_proj.shape[1:], BF16),
        ],
        second, prev, next_, nbt, ids, hidden_proj[0],
        passed=(below[1], above[1]),
        specs=[vmem] * 5 + [anywhere],
        outs=[vmem] * 2 + [anywhere],
        scratch=[pltpu.SemaphoreType.DMA((1,))],
        flops=3 * 10**9,
    )
    hidden_below, hidden_above = from_sides(hidden_copy)
    handed = call(
        halves_kernel, [shape(hidden_proj.shape[2:], BF16)] * 2, *hidden_below, *hidden_above,
        limit=16 * 1024 * 1024, flops=20 * 10**9,
    )
    far = from_far(*handed)
    incoming = lax.all_to_all(
        outgoing.reshape(groups, capacity, width), "elem", split_axis=0, concat_axis=0, tiled=True
    )
    hid = hidden_proj.shape[2]
    tile = 512
    sec = lax.axis_index("sec").astype(jnp.int32).reshape(1)
    (result,) = call(
        functools.partial(network_kernel, tile),
        [shape((slots, width), BF16)],
        sec, incoming.reshape(slots, width), *first, hidden_proj[0], *hidden_above, *far, *hidden_below, *last,
        scratch=[
            pltpu.VMEM((4, *input_proj.shape[1:2], hid // 4), BF16),
            pltpu.VMEM((4, *hidden_proj.shape[1:3], hid // 4), BF16),
            pltpu.VMEM((4, width // 4, hid), BF16),
            pltpu.VMEM((tile, hid), BF16),
            pltpu.VMEM((tile, hid), BF16),
            pltpu.VMEM((slots // tile, tile, width), BF16),
            pltpu.VMEM((slots // tile, tile, width), BF16),
            pltpu.SemaphoreType.DMA((4, 2 + hidden_proj.shape[1])),
            pltpu.SemaphoreType.DMA((slots // tile,)),
            pltpu.SemaphoreType.DMA((slots // tile,)),
        ],
        specs=[pl.BlockSpec(memory_space=pltpu.SMEM)] + [anywhere] * 14,
        outs=[anywhere],
        limit=58 * 1024 * 1024,
        flops=7 * 10**9,
    )
    returned = lax.all_to_all(
        result.reshape(groups, capacity, width), "elem", split_axis=0, concat_axis=0, tiled=True
    )
    (updated,) = call(
        functools.partial(add_kernel, capacity, groups),
        [shape((rows_dev, width), F32)],
        state, returned.reshape(slots, width), ids, flops=10**9,
    )
    return updated.reshape(count, points, width)


def solution(mesh):
    return jax.shard_map(
        on_device,
        mesh=mesh,
        in_specs=(
            P(DEVICE_AXES, None, None),
            P(DEVICE_AXES, None),
            P(),
            P(),
            P(DEVICE_AXES, None),
            P("elem", None, "sec"),
            P("elem", None, None, "sec"),
            P("elem", None, "sec"),
        ),
        out_specs=P(DEVICE_AXES, None, None),
        check_vma=False,
    )
```

```python
import functools

import jax
import jax.numpy as jnp
from jax import lax
from jax.experimental import pallas as pl
from jax.experimental.pallas import tpu as pltpu
from jax.sharding import PartitionSpec as P

F32 = jnp.float32
BF16 = jnp.bfloat16
POINTS = 16
SIDE = 4
DEVICE_AXES = ("elem", "sec")
NT = (((1,), (1,)), ((), ()))
VMEM_LIMIT = 40 * 1024 * 1024


def iota(shape, axis):
    return lax.broadcasted_iota(jnp.int32, shape, axis)


def ones_where(mask):
    return jnp.where(mask, 1.0, 0.0).astype(BF16)


def mul(a, b):
    return jnp.dot(a, b, preferred_element_type=F32)


def mul_nt(a, b):
    return lax.dot_general(a, b, NT, preferred_element_type=F32)


def halves(x):
    high = x.astype(BF16)
    return high, (x - high.astype(F32)).astype(BF16)


def operator_blocks(op):
    size = POINTS * POINTS
    repeat = ones_where((iota((size, POINTS), 0) & (POINTS - 1)) == iota((size, POINTS), 1))
    same = (iota((size, size), 0) >> 4) == (iota((size, size), 1) >> 4)
    blocks = []
    for part in halves(op):
        tall = mul(repeat, part).astype(BF16)
        blocks.append(jnp.where(same, mul_nt(tall, repeat), 0.0).astype(BF16))
    return blocks


def neighbour_columns(nbt):
    count = nbt.shape[1]
    rows = count * POINTS
    spread = ones_where((iota((rows, count), 0) >> 4) == iota((rows, count), 1))
    local = (nbt & (count - 1)).astype(F32).astype(BF16)
    return mul_nt(spread, local)


def near_mask(rows, nbt):
    near = neighbour_columns(nbt)
    place = iota((rows, 1), 0) & (POINTS - 1)
    column = place & (SIDE - 1)
    west = column == 0
    east = column == SIDE - 1
    placef = place.astype(F32)
    source = jnp.where(
        west,
        near[:, 0:1] * POINTS + placef + (SIDE - 1),
        jnp.where(east, near[:, 1:2] * POINTS + placef - (SIDE - 1), -1.0),
    )
    return ones_where(iota((rows, rows), 1).astype(F32) == source), west | east


def advance(state, blocks, rates, mask):
    size = POINTS * POINTS
    op_high, op_low = blocks
    pick, on_edge = mask
    moved = []
    for start in range(0, state.shape[0], size):
        high, low = halves(state[start : start + size])
        moved.append(mul(op_high, high) + (mul(op_high, low) + mul(op_low, high)))
    first = state + rates * jnp.concatenate(moved, axis=0)
    high, low = halves(first)
    far = mul(pick, high) + mul(pick, low)
    return jnp.where(on_edge, 0.5 * (first + far), first)


def edge_rows(shape, axis, first):
    row = iota(shape, axis) + first
    part = row & (POINTS * SIDE - 1)
    element = ((row >> 7) << 4) + (part >> 2)
    return element, (row >> 6) & 1, part & (SIDE - 1)


def edge_advance(state, op, rates, nbt):
    size = POINTS * POINTS
    half = size // 2
    count = nbt.shape[1]
    element, side, place = edge_rows((half, 1), 0, 0)
    point = place + (1 - side) * (POINTS - SIDE)
    here = ones_where(iota((half, size), 1) == element * POINTS + point)
    same = (iota((half, size), 1) >> 4) == element
    rows = ones_where(iota((half, POINTS), 1) == point)
    repeat = ones_where((iota((size, POINTS), 0) & (POINTS - 1)) == iota((size, POINTS), 1))
    op_high, op_low = (
        jnp.where(same, mul_nt(mul(rows, part).astype(BF16), repeat), 0.0).astype(BF16) for part in halves(op)
    )
    first = []
    for start in range(0, state.shape[0], size):
        high, low = halves(state[start : start + size])
        moved = mul(op_high, high) + (mul(op_high, low) + mul(op_low, high))
        first.append(mul(here, high) + mul(here, low) + rates * moved)
    first = jnp.concatenate(first, axis=0)
    total = first.shape[0]
    element, side, place = edge_rows((total, 1), 0, 0)
    spread = ones_where(iota((total, count), 1) == element)
    near = mul_nt(spread, (nbt & (count - 1)).astype(F32).astype(BF16)).astype(jnp.int32)
    west = place == 0
    east = place == SIDE - 1
    other = jnp.where(west, near[:, 0:1], near[:, 1:2])
    there = ((other >> 4) << 7) + (side << 6) + ((other & (POINTS - 1)) << 2) + jnp.where(west, SIDE - 1, 0)
    pick = ones_where(iota((total, total), 1) == jnp.where(west | east, there, -1))
    high, low = halves(first)
    far = mul(pick, high) + mul(pick, low)
    second = jnp.where(west | east, 0.5 * (first + far), first).astype(BF16)
    quarter = half // 2
    north = [second[i : i + quarter] for i in range(0, total, half)]
    south = [second[i + quarter : i + half] for i in range(0, total, half)]
    return jnp.concatenate(north, axis=0), jnp.concatenate(south, axis=0)


def meet(second, below, above, nbt):
    rows = second.shape[0]
    count = below.shape[0]
    near = neighbour_columns(nbt)
    place = iota((rows, 1), 0) & (POINTS - 1)
    south = place < SIDE
    north = place >= POINTS - SIDE
    placef = place.astype(F32)
    source = jnp.where(
        south,
        near[:, 2:3] * SIDE + placef,
        jnp.where(north, near[:, 3:4] * SIDE + placef + (count - (POINTS - SIDE)), -1.0),
    )
    pick = ones_where(iota((rows, 2 * count), 1).astype(F32) == source)
    far = mul(pick, jnp.concatenate([below, above], axis=0))
    return jnp.where(south | north, 0.5 * (second + far), second)


def start_edge_kernel(
    state_ref, nbt_ref, op_ref, rates_ref, north_ref, south_ref, state, nbt, op, rates, sems
):
    pairs = [(state_ref, state), (nbt_ref, nbt), (op_ref, op), (rates_ref, rates)]
    copies = [pltpu.make_async_copy(a, b, sems.at[i]) for i, (a, b) in enumerate(pairs)]
    for copy in copies:
        copy.start()
    for copy in copies:
        copy.wait()
    north_ref[...], south_ref[...] = edge_advance(state[...], op[...], rates[...].reshape(1, -1), nbt[...])


def start_kernel(capacity, groups, state_ref, nbt_ref, op_ref, rates_ref, ids_ref, second_ref, pick_ref):
    state = state_ref[...]
    mask = near_mask(state.shape[0], nbt_ref[...])
    second_ref[...] = advance(state, operator_blocks(op_ref[...]), rates_ref[...].reshape(1, -1), mask)
    rows = state.shape[0]
    named = iota((groups, rows), 0) == ids_ref[...]
    upto = ones_where(iota((rows, rows), 0) <= iota((rows, rows), 1))
    rank = mul(ones_where(named), upto)
    base = (iota((groups, rows), 0) * capacity - 1).astype(F32)
    slot = jnp.sum(jnp.where(named, base + rank, 0.0), axis=0, keepdims=True)
    pick_ref[...] = ones_where(iota((groups * capacity, rows), 0).astype(F32) == slot)


def step_edge_kernel(
    prev_ref, below_ref, above_ref, nbt_ref, op_ref, rates_ref, *refs
):
    north_ref, south_ref = refs[-2:]
    nbt = nbt_ref[...]
    state = meet(prev_ref[...], below_ref[...], above_ref[...], nbt)
    north_ref[...], south_ref[...] = edge_advance(state, op_ref[...], rates_ref[...].reshape(1, -1), nbt)


def step_kernel(prev_ref, below_ref, above_ref, nbt_ref, op_ref, rates_ref, second_ref):
    nbt = nbt_ref[...]
    state = meet(prev_ref[...], below_ref[...], above_ref[...], nbt)
    mask = near_mask(state.shape[0], nbt)
    second_ref[...] = advance(state, operator_blocks(op_ref[...]), rates_ref[...].reshape(1, -1), mask)


def send_kernel(
    prev_ref, below_ref, above_ref, nbt_ref, pick_ref, hidden_ref, *refs
):
    state_ref, out_ref, *copy_refs, sem = refs[-5:]
    hand_on = [pltpu.make_async_copy(hidden_ref.at[i], copy_refs[i], sem.at[i]) for i in range(2)]
    for copy in hand_on:
        copy.start()
    state = meet(prev_ref[...], below_ref[...], above_ref[...], nbt_ref[...])
    state_ref[...] = state
    out_ref[...] = mul(pick_ref[...], state.astype(BF16)).astype(BF16)
    for copy in hand_on:
        copy.wait()


def add_kernel(capacity, groups, state_ref, back_ref, ids_ref, out_ref):
    rows = state_ref.shape[0]
    same = ones_where(iota((rows, rows), 0) == iota((rows, rows), 1))
    ids = jnp.broadcast_to(ids_ref[...].astype(F32).astype(BF16), (8, rows))
    regime = mul_nt(same, ids)[:, 0:1]
    lanes = iota((rows, groups), 1)
    named = lanes.astype(F32) == regime
    upto = ones_where(iota((rows, rows), 1) <= iota((rows, rows), 0))
    rank = mul(upto, ones_where(named))
    base = (lanes * capacity - 1).astype(F32)
    slot = jnp.sum(jnp.where(named, base + rank, 0.0), axis=1, keepdims=True)
    pick = ones_where(iota((rows, groups * capacity), 1).astype(F32) == slot)
    out_ref[...] = state_ref[...] + mul(pick, back_ref[...])


def pass_kernel(in_ref, out_ref):
    pass


def silu(v):
    half = 0.5 * v
    return (half + half * jnp.tanh(half)).astype(BF16)


def network_kernel(tile, sec_ref, rows_ref, *refs):
    first_in, hidden_in, last_in, out_ref = refs[0:4], refs[4:11], refs[11:15], refs[15]
    first, middle, last, hold_a, hold_b, rows, result, sems, row_sems, out_sems = refs[16:]
    layers = middle.shape[1]
    tiles = rows.shape[0]
    places = [(sec_ref[0] + k) & 3 for k in range(4)]
    width = first.shape[2]
    at = [pl.ds(step * tile, tile) for step in range(tiles)]
    incoming = [pltpu.make_async_copy(rows_ref.at[at[i]], rows.at[i], row_sems.at[i]) for i in range(tiles)]
    outgoing = [pltpu.make_async_copy(result.at[i], out_ref.at[at[i]], out_sems.at[i]) for i in range(tiles)]
    weights = [[] for _ in range(layers + 2)]
    for k in range(4):
        pairs = [(first_in[k], first.at[places[k]], 0)]
        for layer in range(layers):
            source = hidden_in[2 * k - 1 + layer] if k else hidden_in[0].at[layer]
            pairs += [(source, middle.at[places[k], layer], 1 + layer)]
        pairs += [(last_in[k], last.at[places[k]], 1 + layers)]
        for source, target, group in pairs:
            weights[group].append(pltpu.make_async_copy(source, target, sems.at[k, group]))
    groups = [[*incoming, *weights[0]], *weights[1:]]

    def begin(group):
        for copy in groups[group]:
            copy.start()

    def arrived(group):
        for copy in groups[group]:
            copy.wait()
        if group + 1 < len(groups):
            begin(group + 1)

    columns = [pl.ds(k * width, width) for k in range(4)]
    begin(0)
    arrived(0)
    for step in range(tiles):
        for k in range(4):
            hold_a[step, :, columns[k]] = silu(mul(rows[step], first[k]))
    now, later = hold_a, hold_b
    for layer in range(layers):
        arrived(1 + layer)
        for step in range(tiles):
            for k in range(4):
                later[step, :, columns[k]] = silu(mul(now[step], middle[k, layer]))
        now, later = later, now
    arrived(1 + layers)
    matrix = last[...].reshape(out_ref.shape[1], now.shape[2])
    for step in range(tiles):
        result[step] = mul_nt(now[step], matrix).astype(BF16)
        outgoing[step].start()
    for copy in outgoing:
        copy.wait()


def call(kernel, out, *args, passed=(), scratch=(), flops=0, specs=None, outs=None, aliases=None, limit=VMEM_LIMIT):
    size = sum(a.size * a.dtype.itemsize for a in args)
    size += sum(o.size * o.dtype.itemsize for o in out)
    vmem = pl.BlockSpec(memory_space=pltpu.VMEM)
    return pl.pallas_call(
        kernel,
        out_shape=[jax.ShapeDtypeStruct(o.shape, o.dtype) for o in out],
        in_specs=(specs or [vmem] * len(args)) + [pl.BlockSpec(memory_space=pl.ANY)] * len(passed),
        out_specs=outs or [vmem] * len(out),
        scratch_shapes=scratch,
        input_output_aliases=aliases or {},
        compiler_params=pltpu.CompilerParams(vmem_limit_bytes=limit),
        cost_estimate=pl.CostEstimate(flops=flops, bytes_accessed=size, transcendentals=0),
    )(*args, *passed)


def ring(count, step):
    return [(i, (i + step) % count) for i in range(count)]


def exchange(north, south):
    total = lax.axis_size(DEVICE_AXES)
    below = lax.ppermute(north, DEVICE_AXES, ring(total, 1))
    above = lax.ppermute(south, DEVICE_AXES, ring(total, -1))
    return below, above


def from_sides(*shards):
    below = [lax.ppermute(x, "sec", ring(4, 1)) for x in shards]
    above = [lax.ppermute(x, "sec", ring(4, -1)) for x in shards]
    return below, above


def from_far(below, above):
    return lax.ppermute(below, "sec", ring(4, 1)), lax.ppermute(above, "sec", ring(4, -1))


def on_device(
    fields, neighbours, operator, rates, regime_ids, input_proj, hidden_proj, output_proj
):
    count, points, width = fields.shape
    rows_dev = count * points
    groups = lax.axis_size("elem")
    capacity = 2 * rows_dev // groups
    slots = groups * capacity
    shape = jax.ShapeDtypeStruct
    nbt = neighbours.T
    ids = regime_ids.T

    mine = (input_proj[0], output_proj[0].T)
    below, above = from_sides(*mine)
    first, last = ([m, a, None, b] for m, a, b in zip(mine, above, below))
    first[2], last[2] = from_far(below[0], above[1])
    anywhere = pl.BlockSpec(memory_space=pl.ANY)
    vmem = pl.BlockSpec(memory_space=pltpu.VMEM)

    edge = shape((count * SIDE, width), BF16)
    inner = shape((rows_dev, width), F32)
    start = fields.reshape(rows_dev, width)
    north, south = call(
        start_edge_kernel, [edge] * 2, start, nbt, operator, rates,
        scratch=[
            pltpu.VMEM((rows_dev, width), F32),
            pltpu.VMEM(nbt.shape, jnp.int32),
            pltpu.VMEM(operator.shape, F32),
            pltpu.VMEM(rates.shape, F32),
            pltpu.SemaphoreType.DMA((4,)),
        ],
        specs=[anywhere] * 4,
        limit=58 * 1024 * 1024,
        flops=2 * 10**9,
    )
    prev, next_ = exchange(north, south)
    second, pick = call(
        functools.partial(start_kernel, capacity, groups),
        [inner, shape((slots, rows_dev), BF16)],
        start, nbt, operator, rates, ids, flops=3 * 10**9,
    )
    step_args = (second, prev, next_, nbt, operator, rates)
    north, south = call(
        step_edge_kernel, [edge] * 2, *step_args, passed=(below[0], above[0]), flops=2 * 10**9
    )
    (second,) = call(step_kernel, [inner], *step_args, flops=3 * 10**9)
    prev, next_ = exchange(north, south)
    state, outgoing, *layer = call(
        send_kernel,
        [
            shape((rows_dev, width), F32),
            shape((slots, width), BF16),
            *[shape(hidden_proj.shape[2:], BF16)] * 2,
        ],
        second, prev, next_, nbt, pick, hidden_proj[0],
        passed=(below[1], above[1]),
        specs=[vmem] * 5 + [anywhere],
        outs=[vmem] * 2 + [anywhere] * 2,
        scratch=[pltpu.SemaphoreType.DMA((2,))],
        flops=3 * 10**9,
    )
    hidden_below, hidden_above = from_sides(*layer)
    (low,) = call(
        pass_kernel, [layer[0]], hidden_below[0],
        specs=[anywhere], outs=[anywhere], aliases={0: 0}, limit=58 * 1024 * 1024, flops=60 * 10**9,
    )
    far = from_far(low, hidden_above[1])
    incoming = lax.all_to_all(
        outgoing.reshape(groups, capacity, width), "elem", split_axis=0, concat_axis=0, tiled=True
    )
    hid = hidden_proj.shape[2]
    tile = 512
    sec = lax.axis_index("sec").astype(jnp.int32).reshape(1)
    (result,) = call(
        functools.partial(network_kernel, tile),
        [shape((slots, width), BF16)],
        sec, incoming.reshape(slots, width), *first, hidden_proj[0], *hidden_above, *far, low, hidden_below[1], *last,
        scratch=[
            pltpu.VMEM((4, *input_proj.shape[1:2], hid // 4), BF16),
            pltpu.VMEM((4, *hidden_proj.shape[1:3], hid // 4), BF16),
            pltpu.VMEM((4, width // 4, hid), BF16),
            pltpu.VMEM((slots // tile, tile, hid), BF16),
            pltpu.VMEM((slots // tile, tile, hid), BF16),
            pltpu.VMEM((slots // tile, tile, width), BF16),
            pltpu.VMEM((slots // tile, tile, width), BF16),
            pltpu.SemaphoreType.DMA((4, 2 + hidden_proj.shape[1])),
            pltpu.SemaphoreType.DMA((slots // tile,)),
            pltpu.SemaphoreType.DMA((slots // tile,)),
        ],
        specs=[pl.BlockSpec(memory_space=pltpu.SMEM)] + [anywhere] * 16,
        outs=[anywhere],
        limit=58 * 1024 * 1024,
        flops=7 * 10**9,
    )
    returned = lax.all_to_all(
        result.reshape(groups, capacity, width), "elem", split_axis=0, concat_axis=0, tiled=True
    )
    (updated,) = call(
        functools.partial(add_kernel, capacity, groups),
        [shape((rows_dev, width), F32)],
        state, returned.reshape(slots, width), ids, flops=10**9,
    )
    return updated.reshape(count, points, width)


def solution(mesh):
    return jax.shard_map(
        on_device,
        mesh=mesh,
        in_specs=(
            P(DEVICE_AXES, None, None),
            P(DEVICE_AXES, None),
            P(),
            P(),
            P(DEVICE_AXES, None),
            P("elem", None, "sec"),
            P("elem", None, None, "sec"),
            P("elem", None, "sec"),
        ),
        out_specs=P(DEVICE_AXES, None, None),
        check_vma=False,
    )
```

```python
import functools

import jax
import jax.numpy as jnp
from jax import lax
from jax.experimental import pallas as pl
from jax.experimental.pallas import tpu as pltpu
from jax.sharding import PartitionSpec as P

F32 = jnp.float32
BF16 = jnp.bfloat16
POINTS = 16
SIDE = 4
DEVICE_AXES = ("elem", "sec")
NT = (((1,), (1,)), ((), ()))
VMEM_LIMIT = 40 * 1024 * 1024


def iota(shape, axis):
    return lax.broadcasted_iota(jnp.int32, shape, axis)


def ones_where(mask):
    return jnp.where(mask, 1.0, 0.0).astype(BF16)


def mul(a, b):
    return jnp.dot(a, b, preferred_element_type=F32)


def mul_nt(a, b):
    return lax.dot_general(a, b, NT, preferred_element_type=F32)


def halves(x):
    high = x.astype(BF16)
    return high, (x - high.astype(F32)).astype(BF16)


def operator_blocks(op):
    size = POINTS * POINTS
    repeat = ones_where((iota((size, POINTS), 0) & (POINTS - 1)) == iota((size, POINTS), 1))
    same = (iota((size, size), 0) >> 4) == (iota((size, size), 1) >> 4)
    blocks = []
    for part in halves(op):
        tall = mul(repeat, part).astype(BF16)
        blocks.append(jnp.where(same, mul_nt(tall, repeat), 0.0).astype(BF16))
    return blocks


def neighbour_columns(nbt):
    count = nbt.shape[1]
    rows = count * POINTS
    spread = ones_where((iota((rows, count), 0) >> 4) == iota((rows, count), 1))
    local = (nbt & (count - 1)).astype(F32).astype(BF16)
    return mul_nt(spread, local)


def near_mask(rows, nbt):
    near = neighbour_columns(nbt)
    place = iota((rows, 1), 0) & (POINTS - 1)
    column = place & (SIDE - 1)
    west = column == 0
    east = column == SIDE - 1
    placef = place.astype(F32)
    source = jnp.where(
        west,
        near[:, 0:1] * POINTS + placef + (SIDE - 1),
        jnp.where(east, near[:, 1:2] * POINTS + placef - (SIDE - 1), -1.0),
    )
    return ones_where(iota((rows, rows), 1).astype(F32) == source), west | east


def advance(state, blocks, rates, mask):
    size = POINTS * POINTS
    op_high, op_low = blocks
    pick, on_edge = mask
    moved = []
    for start in range(0, state.shape[0], size):
        high, low = halves(state[start : start + size])
        moved.append(mul(op_high, high) + (mul(op_high, low) + mul(op_low, high)))
    first = state + rates * jnp.concatenate(moved, axis=0)
    high, low = halves(first)
    far = mul(pick, high) + mul(pick, low)
    return jnp.where(on_edge, 0.5 * (first + far), first)


def edge_rows(shape, axis, first):
    row = iota(shape, axis) + first
    part = row & (POINTS * SIDE - 1)
    element = ((row >> 7) << 4) + (part >> 2)
    return element, (row >> 6) & 1, part & (SIDE - 1)


def edge_advance(state, op, rates, nbt):
    size = POINTS * POINTS
    half = size // 2
    count = nbt.shape[1]
    element, side, place = edge_rows((half, 1), 0, 0)
    point = place + (1 - side) * (POINTS - SIDE)
    here = ones_where(iota((half, size), 1) == element * POINTS + point)
    same = (iota((half, size), 1) >> 4) == element
    rows = ones_where(iota((half, POINTS), 1) == point)
    repeat = ones_where((iota((size, POINTS), 0) & (POINTS - 1)) == iota((size, POINTS), 1))
    op_high, op_low = (
        jnp.where(same, mul_nt(mul(rows, part).astype(BF16), repeat), 0.0).astype(BF16) for part in halves(op)
    )
    first = []
    for start in range(0, state.shape[0], size):
        high, low = halves(state[start : start + size])
        moved = mul(op_high, high) + (mul(op_high, low) + mul(op_low, high))
        first.append(mul(here, high) + mul(here, low) + rates * moved)
    first = jnp.concatenate(first, axis=0)
    total = first.shape[0]
    element, side, place = edge_rows((total, 1), 0, 0)
    spread = ones_where(iota((total, count), 1) == element)
    near = mul_nt(spread, (nbt & (count - 1)).astype(F32).astype(BF16)).astype(jnp.int32)
    west = place == 0
    east = place == SIDE - 1
    other = jnp.where(west, near[:, 0:1], near[:, 1:2])
    there = ((other >> 4) << 7) + (side << 6) + ((other & (POINTS - 1)) << 2) + jnp.where(west, SIDE - 1, 0)
    pick = ones_where(iota((total, total), 1) == jnp.where(west | east, there, -1))
    high, low = halves(first)
    far = mul(pick, high) + mul(pick, low)
    second = jnp.where(west | east, 0.5 * (first + far), first).astype(BF16)
    quarter = half // 2
    north = [second[i : i + quarter] for i in range(0, total, half)]
    south = [second[i + quarter : i + half] for i in range(0, total, half)]
    return jnp.concatenate(north, axis=0), jnp.concatenate(south, axis=0)


def meet(second, below, above, nbt):
    rows = second.shape[0]
    count = below.shape[0]
    near = neighbour_columns(nbt)
    place = iota((rows, 1), 0) & (POINTS - 1)
    south = place < SIDE
    north = place >= POINTS - SIDE
    placef = place.astype(F32)
    source = jnp.where(
        south,
        near[:, 2:3] * SIDE + placef,
        jnp.where(north, near[:, 3:4] * SIDE + placef + (count - (POINTS - SIDE)), -1.0),
    )
    pick = ones_where(iota((rows, 2 * count), 1).astype(F32) == source)
    far = mul(pick, jnp.concatenate([below, above], axis=0))
    return jnp.where(south | north, 0.5 * (second + far), second)


def start_edge_kernel(
    state_ref, nbt_ref, op_ref, rates_ref, north_ref, south_ref, state, nbt, op, rates, sems
):
    pairs = [(state_ref, state), (nbt_ref, nbt), (op_ref, op), (rates_ref, rates)]
    copies = [pltpu.make_async_copy(a, b, sems.at[i]) for i, (a, b) in enumerate(pairs)]
    for copy in copies:
        copy.start()
    for copy in copies:
        copy.wait()
    north_ref[...], south_ref[...] = edge_advance(state[...], op[...], rates[...].reshape(1, -1), nbt[...])


def start_kernel(capacity, groups, state_ref, nbt_ref, op_ref, rates_ref, ids_ref, second_ref, pick_ref):
    state = state_ref[...]
    mask = near_mask(state.shape[0], nbt_ref[...])
    second_ref[...] = advance(state, operator_blocks(op_ref[...]), rates_ref[...].reshape(1, -1), mask)
    rows = state.shape[0]
    named = iota((groups, rows), 0) == ids_ref[...]
    upto = ones_where(iota((rows, rows), 0) <= iota((rows, rows), 1))
    rank = mul(ones_where(named), upto)
    base = (iota((groups, rows), 0) * capacity - 1).astype(F32)
    slot = jnp.sum(jnp.where(named, base + rank, 0.0), axis=0, keepdims=True)
    pick_ref[...] = ones_where(iota((groups * capacity, rows), 0).astype(F32) == slot)


def step_edge_kernel(
    prev_ref, below_ref, above_ref, nbt_ref, op_ref, rates_ref, *refs
):
    north_ref, south_ref = refs[-2:]
    nbt = nbt_ref[...]
    state = meet(prev_ref[...], below_ref[...], above_ref[...], nbt)
    north_ref[...], south_ref[...] = edge_advance(state, op_ref[...], rates_ref[...].reshape(1, -1), nbt)


def step_kernel(prev_ref, below_ref, above_ref, nbt_ref, op_ref, rates_ref, second_ref):
    nbt = nbt_ref[...]
    state = meet(prev_ref[...], below_ref[...], above_ref[...], nbt)
    mask = near_mask(state.shape[0], nbt)
    second_ref[...] = advance(state, operator_blocks(op_ref[...]), rates_ref[...].reshape(1, -1), mask)


def send_kernel(
    prev_ref, below_ref, above_ref, nbt_ref, pick_ref, hidden_ref, *refs
):
    state_ref, out_ref, *copy_refs, sem = refs[-5:]
    hand_on = [pltpu.make_async_copy(hidden_ref.at[i], copy_refs[i], sem.at[i]) for i in range(2)]
    for copy in hand_on:
        copy.start()
    state = meet(prev_ref[...], below_ref[...], above_ref[...], nbt_ref[...])
    state_ref[...] = state
    out_ref[...] = mul(pick_ref[...], state.astype(BF16)).astype(BF16)
    for copy in hand_on:
        copy.wait()


def add_kernel(capacity, groups, state_ref, back_ref, ids_ref, out_ref):
    rows = state_ref.shape[0]
    same = ones_where(iota((rows, rows), 0) == iota((rows, rows), 1))
    ids = jnp.broadcast_to(ids_ref[...].astype(F32).astype(BF16), (8, rows))
    regime = mul_nt(same, ids)[:, 0:1]
    lanes = iota((rows, groups), 1)
    named = lanes.astype(F32) == regime
    upto = ones_where(iota((rows, rows), 1) <= iota((rows, rows), 0))
    rank = mul(upto, ones_where(named))
    base = (lanes * capacity - 1).astype(F32)
    slot = jnp.sum(jnp.where(named, base + rank, 0.0), axis=1, keepdims=True)
    pick = ones_where(iota((rows, groups * capacity), 1).astype(F32) == slot)
    out_ref[...] = state_ref[...] + mul(pick, back_ref[...])


def pass_kernel(*refs):
    pass


def silu(v):
    half = 0.5 * v
    return (half + half * jnp.tanh(half)).astype(BF16)


def network_kernel(tile, sec_ref, rows_ref, *refs):
    first_in, hidden_in, last_in, out_ref = refs[0:4], refs[4:11], refs[11:15], refs[15]
    first, middle, last, hold_a, hold_b, rows, result, sems, row_sems, out_sems = refs[16:]
    layers = middle.shape[1]
    tiles = rows.shape[0]
    places = [(sec_ref[0] + k) & 3 for k in range(4)]
    width = first.shape[2]
    at = [pl.ds(step * tile, tile) for step in range(tiles)]
    incoming = [pltpu.make_async_copy(rows_ref.at[at[i]], rows.at[i], row_sems.at[i]) for i in range(tiles)]
    outgoing = [pltpu.make_async_copy(result.at[i], out_ref.at[at[i]], out_sems.at[i]) for i in range(tiles)]
    weights = [[] for _ in range(layers + 2)]
    for k in range(4):
        pairs = [(first_in[k], first.at[places[k]], 0)]
        for layer in range(layers):
            source = hidden_in[2 * k - 1 + layer] if k else hidden_in[0].at[layer]
            pairs += [(source, middle.at[places[k], layer], 1 + layer)]
        pairs += [(last_in[k], last.at[places[k]], 1 + layers)]
        for source, target, group in pairs:
            weights[group].append(pltpu.make_async_copy(source, target, sems.at[k, group]))
    groups = [[*incoming, *weights[0]], *weights[1:]]

    def begin(group):
        for copy in groups[group]:
            copy.start()

    def arrived(group):
        for copy in groups[group]:
            copy.wait()
        if group + 1 < len(groups):
            begin(group + 1)

    columns = [pl.ds(k * width, width) for k in range(4)]
    begin(0)
    arrived(0)
    for step in range(tiles):
        for k in range(4):
            hold_a[step, :, columns[k]] = silu(mul(rows[step], first[k]))
    now, later = hold_a, hold_b
    for layer in range(layers):
        arrived(1 + layer)
        for step in range(tiles):
            for k in range(4):
                later[step, :, columns[k]] = silu(mul(now[step], middle[k, layer]))
        now, later = later, now
    arrived(1 + layers)
    matrix = last[...].reshape(out_ref.shape[1], now.shape[2])
    for step in range(tiles):
        result[step] = mul_nt(now[step], matrix).astype(BF16)
        outgoing[step].start()
    for copy in outgoing:
        copy.wait()


def call(kernel, out, *args, passed=(), scratch=(), flops=0, specs=None, outs=None, aliases=None, limit=VMEM_LIMIT):
    size = sum(a.size * a.dtype.itemsize for a in args)
    size += sum(o.size * o.dtype.itemsize for o in out)
    vmem = pl.BlockSpec(memory_space=pltpu.VMEM)
    return pl.pallas_call(
        kernel,
        out_shape=[jax.ShapeDtypeStruct(o.shape, o.dtype) for o in out],
        in_specs=(specs or [vmem] * len(args)) + [pl.BlockSpec(memory_space=pl.ANY)] * len(passed),
        out_specs=outs or [vmem] * len(out),
        scratch_shapes=scratch,
        input_output_aliases=aliases or {},
        compiler_params=pltpu.CompilerParams(vmem_limit_bytes=limit),
        cost_estimate=pl.CostEstimate(flops=flops, bytes_accessed=size, transcendentals=0),
    )(*args, *passed)


def ring(count, step):
    return [(i, (i + step) % count) for i in range(count)]


def exchange(north, south):
    total = lax.axis_size(DEVICE_AXES)
    below = lax.ppermute(north, DEVICE_AXES, ring(total, 1))
    above = lax.ppermute(south, DEVICE_AXES, ring(total, -1))
    return below, above


def from_sides(*shards):
    below = [lax.ppermute(x, "sec", ring(4, 1)) for x in shards]
    above = [lax.ppermute(x, "sec", ring(4, -1)) for x in shards]
    return below, above


def from_far(below, above):
    return lax.ppermute(below, "sec", ring(4, 1)), lax.ppermute(above, "sec", ring(4, -1))


def on_device(
    fields, neighbours, operator, rates, regime_ids, input_proj, hidden_proj, output_proj
):
    count, points, width = fields.shape
    rows_dev = count * points
    groups = lax.axis_size("elem")
    capacity = 2 * rows_dev // groups
    slots = groups * capacity
    shape = jax.ShapeDtypeStruct
    nbt = neighbours.T
    ids = regime_ids.T

    mine = (input_proj[0], output_proj[0].T)
    below, above = from_sides(*mine)
    first, last = ([m, a, None, b] for m, a, b in zip(mine, above, below))
    first[2], last[2] = from_far(below[0], above[1])
    anywhere = pl.BlockSpec(memory_space=pl.ANY)
    vmem = pl.BlockSpec(memory_space=pltpu.VMEM)

    edge = shape((count * SIDE, width), BF16)
    inner = shape((rows_dev, width), F32)
    start = fields.reshape(rows_dev, width)
    north, south = call(
        start_edge_kernel, [edge] * 2, start, nbt, operator, rates,
        scratch=[
            pltpu.VMEM((rows_dev, width), F32),
            pltpu.VMEM(nbt.shape, jnp.int32),
            pltpu.VMEM(operator.shape, F32),
            pltpu.VMEM(rates.shape, F32),
            pltpu.SemaphoreType.DMA((4,)),
        ],
        specs=[anywhere] * 4,
        limit=58 * 1024 * 1024,
        flops=2 * 10**9,
    )
    prev, next_ = exchange(north, south)
    second, pick = call(
        functools.partial(start_kernel, capacity, groups),
        [inner, shape((slots, rows_dev), BF16)],
        start, nbt, operator, rates, ids, flops=3 * 10**9,
    )
    step_args = (second, prev, next_, nbt, operator, rates)
    north, south = call(
        step_edge_kernel, [edge] * 2, *step_args, passed=(below[0], above[0]), flops=2 * 10**9
    )
    (second,) = call(step_kernel, [inner], *step_args, flops=3 * 10**9)
    prev, next_ = exchange(north, south)
    state, outgoing, *layer = call(
        send_kernel,
        [
            shape((rows_dev, width), F32),
            shape((slots, width), BF16),
            *[shape(hidden_proj.shape[2:], BF16)] * 2,
        ],
        second, prev, next_, nbt, pick, hidden_proj[0],
        passed=(below[1], above[1]),
        specs=[vmem] * 5 + [anywhere],
        outs=[vmem] * 2 + [anywhere] * 2,
        scratch=[pltpu.SemaphoreType.DMA((2,))],
        flops=3 * 10**9,
    )
    hidden_below, hidden_above = from_sides(*layer)
    low_below, low_above = call(
        pass_kernel, [layer[0]] * 2, hidden_below[0], hidden_above[0],
        specs=[anywhere] * 2, outs=[anywhere] * 2, aliases={0: 0, 1: 1}, limit=58 * 1024 * 1024, flops=22 * 10**9,
    )
    far = from_far(low_below, hidden_above[1])
    incoming = lax.all_to_all(
        outgoing.reshape(groups, capacity, width), "elem", split_axis=0, concat_axis=0, tiled=True
    )
    hid = hidden_proj.shape[2]
    tile = 512
    sec = lax.axis_index("sec").astype(jnp.int32).reshape(1)
    (result,) = call(
        functools.partial(network_kernel, tile),
        [shape((slots, width), BF16)],
        sec, incoming.reshape(slots, width), *first, hidden_proj[0], low_above, hidden_above[1], *far, low_below, hidden_below[1], *last,
        scratch=[
            pltpu.VMEM((4, *input_proj.shape[1:2], hid // 4), BF16),
            pltpu.VMEM((4, *hidden_proj.shape[1:3], hid // 4), BF16),
            pltpu.VMEM((4, width // 4, hid), BF16),
            pltpu.VMEM((slots // tile, tile, hid), BF16),
            pltpu.VMEM((slots // tile, tile, hid), BF16),
            pltpu.VMEM((slots // tile, tile, width), BF16),
            pltpu.VMEM((slots // tile, tile, width), BF16),
            pltpu.SemaphoreType.DMA((4, 2 + hidden_proj.shape[1])),
            pltpu.SemaphoreType.DMA((slots // tile,)),
            pltpu.SemaphoreType.DMA((slots // tile,)),
        ],
        specs=[pl.BlockSpec(memory_space=pltpu.SMEM)] + [anywhere] * 16,
        outs=[anywhere],
        limit=58 * 1024 * 1024,
        flops=7 * 10**9,
    )
    returned = lax.all_to_all(
        result.reshape(groups, capacity, width), "elem", split_axis=0, concat_axis=0, tiled=True
    )
    (updated,) = call(
        functools.partial(add_kernel, capacity, groups),
        [shape((rows_dev, width), F32)],
        state, returned.reshape(slots, width), ids, flops=10**9,
    )
    return updated.reshape(count, points, width)


def solution(mesh):
    return jax.shard_map(
        on_device,
        mesh=mesh,
        in_specs=(
            P(DEVICE_AXES, None, None),
            P(DEVICE_AXES, None),
            P(),
            P(),
            P(DEVICE_AXES, None),
            P("elem", None, "sec"),
            P("elem", None, None, "sec"),
            P("elem", None, "sec"),
        ),
        out_specs=P(DEVICE_AXES, None, None),
        check_vma=False,
    )
```

```python
import functools

import jax
import jax.numpy as jnp
from jax import lax
from jax.experimental import pallas as pl
from jax.experimental.pallas import tpu as pltpu
from jax.sharding import PartitionSpec as P

F32 = jnp.float32
BF16 = jnp.bfloat16
POINTS = 16
SIDE = 4
DEVICE_AXES = ("elem", "sec")
NT = (((1,), (1,)), ((), ()))
VMEM_LIMIT = 40 * 1024 * 1024


def iota(shape, axis):
    return lax.broadcasted_iota(jnp.int32, shape, axis)


def ones_where(mask):
    return jnp.where(mask, 1.0, 0.0).astype(BF16)


def mul(a, b):
    return jnp.dot(a, b, preferred_element_type=F32)


def mul_nt(a, b):
    return lax.dot_general(a, b, NT, preferred_element_type=F32)


def halves(x):
    high = x.astype(BF16)
    return high, (x - high.astype(F32)).astype(BF16)


def operator_blocks(op):
    size = POINTS * POINTS
    repeat = ones_where((iota((size, POINTS), 0) & (POINTS - 1)) == iota((size, POINTS), 1))
    same = (iota((size, size), 0) >> 4) == (iota((size, size), 1) >> 4)
    blocks = []
    for part in halves(op):
        tall = mul(repeat, part).astype(BF16)
        blocks.append(jnp.where(same, mul_nt(tall, repeat), 0.0).astype(BF16))
    return blocks


def neighbour_columns(nbt):
    count = nbt.shape[1]
    rows = count * POINTS
    spread = ones_where((iota((rows, count), 0) >> 4) == iota((rows, count), 1))
    local = (nbt & (count - 1)).astype(F32).astype(BF16)
    return mul_nt(spread, local)


def near_mask(rows, nbt):
    near = neighbour_columns(nbt)
    place = iota((rows, 1), 0) & (POINTS - 1)
    column = place & (SIDE - 1)
    west = column == 0
    east = column == SIDE - 1
    placef = place.astype(F32)
    source = jnp.where(
        west,
        near[:, 0:1] * POINTS + placef + (SIDE - 1),
        jnp.where(east, near[:, 1:2] * POINTS + placef - (SIDE - 1), -1.0),
    )
    return ones_where(iota((rows, rows), 1).astype(F32) == source), west | east


def advance(state, blocks, rates, mask):
    size = POINTS * POINTS
    op_high, op_low = blocks
    pick, on_edge = mask
    moved = []
    for start in range(0, state.shape[0], size):
        high, low = halves(state[start : start + size])
        moved.append(mul(op_high, high) + (mul(op_high, low) + mul(op_low, high)))
    first = state + rates * jnp.concatenate(moved, axis=0)
    high, low = halves(first)
    far = mul(pick, high) + mul(pick, low)
    return jnp.where(on_edge, 0.5 * (first + far), first)


def edge_rows(shape, axis, first):
    row = iota(shape, axis) + first
    part = row & (POINTS * SIDE - 1)
    element = ((row >> 7) << 4) + (part >> 2)
    return element, (row >> 6) & 1, part & (SIDE - 1)


def edge_advance(state, op, rates, nbt):
    size = POINTS * POINTS
    half = size // 2
    count = nbt.shape[1]
    element, side, place = edge_rows((half, 1), 0, 0)
    point = place + (1 - side) * (POINTS - SIDE)
    here = ones_where(iota((half, size), 1) == element * POINTS + point)
    same = (iota((half, size), 1) >> 4) == element
    rows = ones_where(iota((half, POINTS), 1) == point)
    repeat = ones_where((iota((size, POINTS), 0) & (POINTS - 1)) == iota((size, POINTS), 1))
    op_high, op_low = (
        jnp.where(same, mul_nt(mul(rows, part).astype(BF16), repeat), 0.0).astype(BF16) for part in halves(op)
    )
    first = []
    for start in range(0, state.shape[0], size):
        high, low = halves(state[start : start + size])
        moved = mul(op_high, high) + (mul(op_high, low) + mul(op_low, high))
        first.append(mul(here, high) + mul(here, low) + rates * moved)
    first = jnp.concatenate(first, axis=0)
    total = first.shape[0]
    element, side, place = edge_rows((total, 1), 0, 0)
    spread = ones_where(iota((total, count), 1) == element)
    near = mul_nt(spread, (nbt & (count - 1)).astype(F32).astype(BF16)).astype(jnp.int32)
    west = place == 0
    east = place == SIDE - 1
    other = jnp.where(west, near[:, 0:1], near[:, 1:2])
    there = ((other >> 4) << 7) + (side << 6) + ((other & (POINTS - 1)) << 2) + jnp.where(west, SIDE - 1, 0)
    pick = ones_where(iota((total, total), 1) == jnp.where(west | east, there, -1))
    high, low = halves(first)
    far = mul(pick, high) + mul(pick, low)
    second = jnp.where(west | east, 0.5 * (first + far), first).astype(BF16)
    quarter = half // 2
    north = [second[i : i + quarter] for i in range(0, total, half)]
    south = [second[i + quarter : i + half] for i in range(0, total, half)]
    return jnp.concatenate(north, axis=0), jnp.concatenate(south, axis=0)


def meet(second, below, above, nbt):
    rows = second.shape[0]
    count = below.shape[0]
    near = neighbour_columns(nbt)
    place = iota((rows, 1), 0) & (POINTS - 1)
    south = place < SIDE
    north = place >= POINTS - SIDE
    placef = place.astype(F32)
    source = jnp.where(
        south,
        near[:, 2:3] * SIDE + placef,
        jnp.where(north, near[:, 3:4] * SIDE + placef + (count - (POINTS - SIDE)), -1.0),
    )
    pick = ones_where(iota((rows, 2 * count), 1).astype(F32) == source)
    far = mul(pick, jnp.concatenate([below, above], axis=0))
    return jnp.where(south | north, 0.5 * (second + far), second)


def start_edge_kernel(
    state_ref, nbt_ref, op_ref, rates_ref, north_ref, south_ref, state, nbt, op, rates, sems
):
    pairs = [(state_ref, state), (nbt_ref, nbt), (op_ref, op), (rates_ref, rates)]
    copies = [pltpu.make_async_copy(a, b, sems.at[i]) for i, (a, b) in enumerate(pairs)]
    for copy in copies:
        copy.start()
    for copy in copies:
        copy.wait()
    north_ref[...], south_ref[...] = edge_advance(state[...], op[...], rates[...].reshape(1, -1), nbt[...])


def start_kernel(capacity, groups, state_ref, nbt_ref, op_ref, rates_ref, ids_ref, second_ref, pick_ref):
    state = state_ref[...]
    mask = near_mask(state.shape[0], nbt_ref[...])
    second_ref[...] = advance(state, operator_blocks(op_ref[...]), rates_ref[...].reshape(1, -1), mask)
    rows = state.shape[0]
    named = iota((groups, rows), 0) == ids_ref[...]
    upto = ones_where(iota((rows, rows), 0) <= iota((rows, rows), 1))
    rank = mul(ones_where(named), upto)
    base = (iota((groups, rows), 0) * capacity - 1).astype(F32)
    slot = jnp.sum(jnp.where(named, base + rank, 0.0), axis=0, keepdims=True)
    pick_ref[...] = ones_where(iota((groups * capacity, rows), 0).astype(F32) == slot)


def step_edge_kernel(
    prev_ref, below_ref, above_ref, nbt_ref, op_ref, rates_ref, *refs
):
    north_ref, south_ref = refs[-2:]
    nbt = nbt_ref[...]
    state = meet(prev_ref[...], below_ref[...], above_ref[...], nbt)
    north_ref[...], south_ref[...] = edge_advance(state, op_ref[...], rates_ref[...].reshape(1, -1), nbt)


def step_kernel(prev_ref, below_ref, above_ref, nbt_ref, op_ref, rates_ref, second_ref):
    nbt = nbt_ref[...]
    state = meet(prev_ref[...], below_ref[...], above_ref[...], nbt)
    mask = near_mask(state.shape[0], nbt)
    second_ref[...] = advance(state, operator_blocks(op_ref[...]), rates_ref[...].reshape(1, -1), mask)


def send_kernel(
    prev_ref, below_ref, above_ref, nbt_ref, pick_ref, hidden_ref, *refs
):
    state_ref, out_ref, *copy_refs, sem = refs[-5:]
    hand_on = [pltpu.make_async_copy(hidden_ref.at[i], copy_refs[i], sem.at[i]) for i in range(2)]
    for copy in hand_on:
        copy.start()
    state = meet(prev_ref[...], below_ref[...], above_ref[...], nbt_ref[...])
    state_ref[...] = state
    out_ref[...] = mul(pick_ref[...], state.astype(BF16)).astype(BF16)
    for copy in hand_on:
        copy.wait()


def add_kernel(capacity, groups, state_ref, back_ref, ids_ref, out_ref):
    rows = state_ref.shape[0]
    same = ones_where(iota((rows, rows), 0) == iota((rows, rows), 1))
    ids = jnp.broadcast_to(ids_ref[...].astype(F32).astype(BF16), (8, rows))
    regime = mul_nt(same, ids)[:, 0:1]
    lanes = iota((rows, groups), 1)
    named = lanes.astype(F32) == regime
    upto = ones_where(iota((rows, rows), 1) <= iota((rows, rows), 0))
    rank = mul(upto, ones_where(named))
    base = (lanes * capacity - 1).astype(F32)
    slot = jnp.sum(jnp.where(named, base + rank, 0.0), axis=1, keepdims=True)
    pick = ones_where(iota((rows, groups * capacity), 1).astype(F32) == slot)
    out_ref[...] = state_ref[...] + mul(pick, back_ref[...])


def pass_kernel(*refs):
    pass


def silu(v):
    half = 0.5 * v
    return (half + half * jnp.tanh(half)).astype(BF16)


def network_kernel(tile, sec_ref, rows_ref, *refs):
    first_in, hidden_in, last_in, out_ref = refs[0:4], refs[4:11], refs[11:15], refs[15]
    first, middle, last, hold_a, hold_b, rows, result, sems, row_sems, out_sems = refs[16:]
    layers = middle.shape[1]
    tiles = rows.shape[0]
    places = [(sec_ref[0] + k) & 3 for k in range(4)]
    width = first.shape[2]
    at = [pl.ds(step * tile, tile) for step in range(tiles)]
    incoming = [pltpu.make_async_copy(rows_ref.at[at[i]], rows.at[i], row_sems.at[i]) for i in range(tiles)]
    outgoing = [pltpu.make_async_copy(result.at[i], out_ref.at[at[i]], out_sems.at[i]) for i in range(tiles)]
    weights = [[] for _ in range(layers + 2)]
    for k in range(4):
        pairs = [(first_in[k], first.at[places[k]], 0)]
        for layer in range(layers):
            source = hidden_in[2 * k - 1 + layer] if k else hidden_in[0].at[layer]
            pairs += [(source, middle.at[places[k], layer], 1 + layer)]
        pairs += [(last_in[k], last.at[places[k]], 1 + layers)]
        for source, target, group in pairs:
            weights[group].append(pltpu.make_async_copy(source, target, sems.at[k, group]))
    groups = [[*incoming, *weights[0]], *weights[1:]]

    def begin(group):
        for copy in groups[group]:
            copy.start()

    def arrived(group):
        for copy in groups[group]:
            copy.wait()
        if group + 1 < len(groups):
            begin(group + 1)

    columns = [pl.ds(k * width, width) for k in range(4)]
    begin(0)
    arrived(0)
    for step in range(tiles):
        for k in range(4):
            hold_a[step, :, columns[k]] = silu(mul(rows[step], first[k]))
    now, later = hold_a, hold_b
    for layer in range(layers):
        arrived(1 + layer)
        for step in range(tiles):
            for k in range(4):
                later[step, :, columns[k]] = silu(mul(now[step], middle[k, layer]))
        now, later = later, now
    arrived(1 + layers)
    matrix = last[...].reshape(out_ref.shape[1], now.shape[2])
    for step in range(tiles):
        result[step] = mul_nt(now[step], matrix).astype(BF16)
        outgoing[step].start()
    for copy in outgoing:
        copy.wait()


def call(kernel, out, *args, passed=(), scratch=(), flops=0, specs=None, outs=None, aliases=None, limit=VMEM_LIMIT):
    size = sum(a.size * a.dtype.itemsize for a in args)
    size += sum(o.size * o.dtype.itemsize for o in out)
    vmem = pl.BlockSpec(memory_space=pltpu.VMEM)
    return pl.pallas_call(
        kernel,
        out_shape=[jax.ShapeDtypeStruct(o.shape, o.dtype) for o in out],
        in_specs=(specs or [vmem] * len(args)) + [pl.BlockSpec(memory_space=pl.ANY)] * len(passed),
        out_specs=outs or [vmem] * len(out),
        scratch_shapes=scratch,
        input_output_aliases=aliases or {},
        compiler_params=pltpu.CompilerParams(vmem_limit_bytes=limit),
        cost_estimate=pl.CostEstimate(flops=flops, bytes_accessed=size, transcendentals=0),
    )(*args, *passed)


def ring(count, step):
    return [(i, (i + step) % count) for i in range(count)]


def exchange(north, south):
    total = lax.axis_size(DEVICE_AXES)
    below = lax.ppermute(north, DEVICE_AXES, ring(total, 1))
    above = lax.ppermute(south, DEVICE_AXES, ring(total, -1))
    return below, above


def from_sides(*shards):
    below = [lax.ppermute(x, "sec", ring(4, 1)) for x in shards]
    above = [lax.ppermute(x, "sec", ring(4, -1)) for x in shards]
    return below, above


def from_far(below, above):
    return lax.ppermute(below, "sec", ring(4, 1)), lax.ppermute(above, "sec", ring(4, -1))


def on_device(
    fields, neighbours, operator, rates, regime_ids, input_proj, hidden_proj, output_proj
):
    count, points, width = fields.shape
    rows_dev = count * points
    groups = lax.axis_size("elem")
    capacity = 2 * rows_dev // groups
    slots = groups * capacity
    shape = jax.ShapeDtypeStruct
    nbt = neighbours.T
    ids = regime_ids.T

    mine = (input_proj[0], output_proj[0].T)
    below, above = from_sides(*mine)
    first, last = ([m, a, None, b] for m, a, b in zip(mine, above, below))
    ends_far = from_far(below[0], above[1])
    anywhere = pl.BlockSpec(memory_space=pl.ANY)
    vmem = pl.BlockSpec(memory_space=pltpu.VMEM)

    edge = shape((count * SIDE, width), BF16)
    inner = shape((rows_dev, width), F32)
    start = fields.reshape(rows_dev, width)
    north, south = call(
        start_edge_kernel, [edge] * 2, start, nbt, operator, rates,
        scratch=[
            pltpu.VMEM((rows_dev, width), F32),
            pltpu.VMEM(nbt.shape, jnp.int32),
            pltpu.VMEM(operator.shape, F32),
            pltpu.VMEM(rates.shape, F32),
            pltpu.SemaphoreType.DMA((4,)),
        ],
        specs=[anywhere] * 4,
        limit=58 * 1024 * 1024,
        flops=2 * 10**9,
    )
    prev, next_ = exchange(north, south)
    second, pick = call(
        functools.partial(start_kernel, capacity, groups),
        [inner, shape((slots, rows_dev), BF16)],
        start, nbt, operator, rates, ids, flops=3 * 10**9,
    )
    step_args = (second, prev, next_, nbt, operator, rates)
    north, south = call(
        step_edge_kernel, [edge] * 2, *step_args, passed=(below[0], above[0]), flops=2 * 10**9
    )
    (second,) = call(step_kernel, [inner], *step_args, flops=3 * 10**9)
    prev, next_ = exchange(north, south)
    state, outgoing, *layer = call(
        send_kernel,
        [
            shape((rows_dev, width), F32),
            shape((slots, width), BF16),
            *[shape(hidden_proj.shape[2:], BF16)] * 2,
        ],
        second, prev, next_, nbt, pick, hidden_proj[0],
        passed=(below[1], above[1]),
        specs=[vmem] * 5 + [anywhere],
        outs=[vmem] * 2 + [anywhere] * 2,
        scratch=[pltpu.SemaphoreType.DMA((2,))],
        flops=3 * 10**9,
    )
    hidden_below, hidden_above = from_sides(*layer)
    low_below, low_above = call(
        pass_kernel, [layer[0]] * 2, hidden_below[0], hidden_above[0],
        specs=[anywhere] * 2, outs=[anywhere] * 2, aliases={0: 0, 1: 1}, limit=58 * 1024 * 1024, flops=19 * 10**9,
    )
    far = from_far(low_below, hidden_above[1])
    first[2], last[2] = call(
        pass_kernel, ends_far, *ends_far,
        specs=[anywhere] * 2, outs=[anywhere] * 2, aliases={0: 0, 1: 1}, limit=58 * 1024 * 1024, flops=10 * 10**9,
    )
    incoming = lax.all_to_all(
        outgoing.reshape(groups, capacity, width), "elem", split_axis=0, concat_axis=0, tiled=True
    )
    hid = hidden_proj.shape[2]
    tile = 512
    sec = lax.axis_index("sec").astype(jnp.int32).reshape(1)
    (result,) = call(
        functools.partial(network_kernel, tile),
        [shape((slots, width), BF16)],
        sec, incoming.reshape(slots, width), *first, hidden_proj[0], low_above, hidden_above[1], *far, low_below, hidden_below[1], *last,
        scratch=[
            pltpu.VMEM((4, *input_proj.shape[1:2], hid // 4), BF16),
            pltpu.VMEM((4, *hidden_proj.shape[1:3], hid // 4), BF16),
            pltpu.VMEM((4, width // 4, hid), BF16),
            pltpu.VMEM((slots // tile, tile, hid), BF16),
            pltpu.VMEM((slots // tile, tile, hid), BF16),
            pltpu.VMEM((slots // tile, tile, width), BF16),
            pltpu.VMEM((slots // tile, tile, width), BF16),
            pltpu.SemaphoreType.DMA((4, 2 + hidden_proj.shape[1])),
            pltpu.SemaphoreType.DMA((slots // tile,)),
            pltpu.SemaphoreType.DMA((slots // tile,)),
        ],
        specs=[pl.BlockSpec(memory_space=pltpu.SMEM)] + [anywhere] * 16,
        outs=[anywhere],
        limit=58 * 1024 * 1024,
        flops=7 * 10**9,
    )
    returned = lax.all_to_all(
        result.reshape(groups, capacity, width), "elem", split_axis=0, concat_axis=0, tiled=True
    )
    (updated,) = call(
        functools.partial(add_kernel, capacity, groups),
        [shape((rows_dev, width), F32)],
        state, returned.reshape(slots, width), ids, flops=10**9,
    )
    return updated.reshape(count, points, width)


def solution(mesh):
    return jax.shard_map(
        on_device,
        mesh=mesh,
        in_specs=(
            P(DEVICE_AXES, None, None),
            P(DEVICE_AXES, None),
            P(),
            P(),
            P(DEVICE_AXES, None),
            P("elem", None, "sec"),
            P("elem", None, None, "sec"),
            P("elem", None, "sec"),
        ),
        out_specs=P(DEVICE_AXES, None, None),
        check_vma=False,
    )
```

```python
import functools

import jax
import jax.numpy as jnp
from jax import lax
from jax.experimental import pallas as pl
from jax.experimental.pallas import tpu as pltpu
from jax.sharding import PartitionSpec as P

F32 = jnp.float32
BF16 = jnp.bfloat16
POINTS = 16
SIDE = 4
DEVICE_AXES = ("elem", "sec")
NT = (((1,), (1,)), ((), ()))
VMEM_LIMIT = 40 * 1024 * 1024


def iota(shape, axis):
    return lax.broadcasted_iota(jnp.int32, shape, axis)


def ones_where(mask):
    return jnp.where(mask, 1.0, 0.0).astype(BF16)


def mul(a, b):
    return jnp.dot(a, b, preferred_element_type=F32)


def mul_nt(a, b):
    return lax.dot_general(a, b, NT, preferred_element_type=F32)


def halves(x):
    high = x.astype(BF16)
    return high, (x - high.astype(F32)).astype(BF16)


def operator_blocks(op):
    size = POINTS * POINTS
    repeat = ones_where((iota((size, POINTS), 0) & (POINTS - 1)) == iota((size, POINTS), 1))
    same = (iota((size, size), 0) >> 4) == (iota((size, size), 1) >> 4)
    blocks = []
    for part in halves(op):
        tall = mul(repeat, part).astype(BF16)
        blocks.append(jnp.where(same, mul_nt(tall, repeat), 0.0).astype(BF16))
    return blocks


def neighbour_columns(nbt):
    count = nbt.shape[1]
    rows = count * POINTS
    spread = ones_where((iota((rows, count), 0) >> 4) == iota((rows, count), 1))
    local = (nbt & (count - 1)).astype(F32).astype(BF16)
    return mul_nt(spread, local)


def near_mask(rows, nbt):
    near = neighbour_columns(nbt)
    place = iota((rows, 1), 0) & (POINTS - 1)
    column = place & (SIDE - 1)
    west = column == 0
    east = column == SIDE - 1
    placef = place.astype(F32)
    source = jnp.where(
        west,
        near[:, 0:1] * POINTS + placef + (SIDE - 1),
        jnp.where(east, near[:, 1:2] * POINTS + placef - (SIDE - 1), -1.0),
    )
    return ones_where(iota((rows, rows), 1).astype(F32) == source), west | east


def advance(state, blocks, rates, mask):
    size = POINTS * POINTS
    op_high, op_low = blocks
    pick, on_edge = mask
    moved = []
    for start in range(0, state.shape[0], size):
        high, low = halves(state[start : start + size])
        moved.append(mul(op_high, high) + (mul(op_high, low) + mul(op_low, high)))
    first = state + rates * jnp.concatenate(moved, axis=0)
    high, low = halves(first)
    far = mul(pick, high) + mul(pick, low)
    return jnp.where(on_edge, 0.5 * (first + far), first)


def edge_rows(shape, axis, first):
    row = iota(shape, axis) + first
    part = row & (POINTS * SIDE - 1)
    element = ((row >> 7) << 4) + (part >> 2)
    return element, (row >> 6) & 1, part & (SIDE - 1)


def edge_advance(state, op, rates, nbt):
    size = POINTS * POINTS
    half = size // 2
    count = nbt.shape[1]
    element, side, place = edge_rows((half, 1), 0, 0)
    point = place + (1 - side) * (POINTS - SIDE)
    here = ones_where(iota((half, size), 1) == element * POINTS + point)
    same = (iota((half, size), 1) >> 4) == element
    rows = ones_where(iota((half, POINTS), 1) == point)
    repeat = ones_where((iota((size, POINTS), 0) & (POINTS - 1)) == iota((size, POINTS), 1))
    op_high, op_low = (
        jnp.where(same, mul_nt(mul(rows, part).astype(BF16), repeat), 0.0).astype(BF16) for part in halves(op)
    )
    first = []
    for start in range(0, state.shape[0], size):
        high, low = halves(state[start : start + size])
        moved = mul(op_high, high) + (mul(op_high, low) + mul(op_low, high))
        first.append(mul(here, high) + mul(here, low) + rates * moved)
    first = jnp.concatenate(first, axis=0)
    total = first.shape[0]
    element, side, place = edge_rows((total, 1), 0, 0)
    spread = ones_where(iota((total, count), 1) == element)
    near = mul_nt(spread, (nbt & (count - 1)).astype(F32).astype(BF16)).astype(jnp.int32)
    west = place == 0
    east = place == SIDE - 1
    other = jnp.where(west, near[:, 0:1], near[:, 1:2])
    there = ((other >> 4) << 7) + (side << 6) + ((other & (POINTS - 1)) << 2) + jnp.where(west, SIDE - 1, 0)
    pick = ones_where(iota((total, total), 1) == jnp.where(west | east, there, -1))
    far = mul(pick, first.astype(BF16))
    second = jnp.where(west | east, 0.5 * (first + far), first).astype(BF16)
    quarter = half // 2
    north = [second[i : i + quarter] for i in range(0, total, half)]
    south = [second[i + quarter : i + half] for i in range(0, total, half)]
    return jnp.concatenate(north, axis=0), jnp.concatenate(south, axis=0)


def meet(second, below, above, nbt):
    rows = second.shape[0]
    count = below.shape[0]
    near = neighbour_columns(nbt)
    place = iota((rows, 1), 0) & (POINTS - 1)
    south = place < SIDE
    north = place >= POINTS - SIDE
    placef = place.astype(F32)
    source = jnp.where(
        south,
        near[:, 2:3] * SIDE + placef,
        jnp.where(north, near[:, 3:4] * SIDE + placef + (count - (POINTS - SIDE)), -1.0),
    )
    pick = ones_where(iota((rows, 2 * count), 1).astype(F32) == source)
    far = mul(pick, jnp.concatenate([below, above], axis=0))
    return jnp.where(south | north, 0.5 * (second + far), second)


def start_edge_kernel(
    state_ref, nbt_ref, op_ref, rates_ref, north_ref, south_ref, state, nbt, op, rates, sems
):
    pairs = [(state_ref, state), (nbt_ref, nbt), (op_ref, op), (rates_ref, rates)]
    copies = [pltpu.make_async_copy(a, b, sems.at[i]) for i, (a, b) in enumerate(pairs)]
    for copy in copies:
        copy.start()
    for copy in copies:
        copy.wait()
    north_ref[...], south_ref[...] = edge_advance(state[...], op[...], rates[...].reshape(1, -1), nbt[...])


def start_kernel(capacity, groups, state_ref, nbt_ref, op_ref, rates_ref, ids_ref, second_ref, pick_ref):
    state = state_ref[...]
    mask = near_mask(state.shape[0], nbt_ref[...])
    second_ref[...] = advance(state, operator_blocks(op_ref[...]), rates_ref[...].reshape(1, -1), mask)
    rows = state.shape[0]
    named = iota((groups, rows), 0) == ids_ref[...]
    upto = ones_where(iota((rows, rows), 0) <= iota((rows, rows), 1))
    rank = mul(ones_where(named), upto)
    base = (iota((groups, rows), 0) * capacity - 1).astype(F32)
    slot = jnp.sum(jnp.where(named, base + rank, 0.0), axis=0, keepdims=True)
    pick_ref[...] = ones_where(iota((groups * capacity, rows), 0).astype(F32) == slot)


def step_edge_kernel(
    prev_ref, below_ref, above_ref, nbt_ref, op_ref, rates_ref, *refs
):
    north_ref, south_ref = refs[-2:]
    nbt = nbt_ref[...]
    state = meet(prev_ref[...], below_ref[...], above_ref[...], nbt)
    north_ref[...], south_ref[...] = edge_advance(state, op_ref[...], rates_ref[...].reshape(1, -1), nbt)


def step_kernel(prev_ref, below_ref, above_ref, nbt_ref, op_ref, rates_ref, second_ref):
    nbt = nbt_ref[...]
    state = meet(prev_ref[...], below_ref[...], above_ref[...], nbt)
    mask = near_mask(state.shape[0], nbt)
    second_ref[...] = advance(state, operator_blocks(op_ref[...]), rates_ref[...].reshape(1, -1), mask)


def send_kernel(
    prev_ref, below_ref, above_ref, nbt_ref, pick_ref, hidden_ref, *refs
):
    state_ref, out_ref, *copy_refs, sem = refs[-5:]
    hand_on = [pltpu.make_async_copy(hidden_ref.at[i], copy_refs[i], sem.at[i]) for i in range(2)]
    for copy in hand_on:
        copy.start()
    state = meet(prev_ref[...], below_ref[...], above_ref[...], nbt_ref[...])
    state_ref[...] = state
    out_ref[...] = mul(pick_ref[...], state.astype(BF16)).astype(BF16)
    for copy in hand_on:
        copy.wait()


def add_kernel(capacity, groups, state_ref, back_ref, ids_ref, out_ref):
    rows = state_ref.shape[0]
    same = ones_where(iota((rows, rows), 0) == iota((rows, rows), 1))
    ids = jnp.broadcast_to(ids_ref[...].astype(F32).astype(BF16), (8, rows))
    regime = mul_nt(same, ids)[:, 0:1]
    lanes = iota((rows, groups), 1)
    named = lanes.astype(F32) == regime
    upto = ones_where(iota((rows, rows), 1) <= iota((rows, rows), 0))
    rank = mul(upto, ones_where(named))
    base = (lanes * capacity - 1).astype(F32)
    slot = jnp.sum(jnp.where(named, base + rank, 0.0), axis=1, keepdims=True)
    pick = ones_where(iota((rows, groups * capacity), 1).astype(F32) == slot)
    out_ref[...] = state_ref[...] + mul(pick, back_ref[...])


def pass_kernel(*refs):
    pass


def silu(v):
    half = 0.5 * v
    return (half + half * jnp.tanh(half)).astype(BF16)


def network_kernel(tile, sec_ref, rows_ref, *refs):
    first_in, hidden_in, last_in, out_ref = refs[0:4], refs[4:11], refs[11:15], refs[15]
    first, middle, last, hold_a, hold_b, rows, result, sems, row_sems, out_sems = refs[16:]
    layers = middle.shape[1]
    tiles = rows.shape[0]
    places = [(sec_ref[0] + k) & 3 for k in range(4)]
    width = first.shape[2]
    at = [pl.ds(step * tile, tile) for step in range(tiles)]
    incoming = [pltpu.make_async_copy(rows_ref.at[at[i]], rows.at[i], row_sems.at[i]) for i in range(tiles)]
    outgoing = [pltpu.make_async_copy(result.at[i], out_ref.at[at[i]], out_sems.at[i]) for i in range(tiles)]
    weights = [[] for _ in range(layers + 2)]
    for k in range(4):
        pairs = [(first_in[k], first.at[places[k]], 0)]
        for layer in range(layers):
            source = hidden_in[2 * k - 1 + layer] if k else hidden_in[0].at[layer]
            pairs += [(source, middle.at[places[k], layer], 1 + layer)]
        pairs += [(last_in[k], last.at[places[k]], 1 + layers)]
        for source, target, group in pairs:
            weights[group].append(pltpu.make_async_copy(source, target, sems.at[k, group]))
    groups = [[*incoming, *weights[0]], *weights[1:]]

    def begin(group):
        for copy in groups[group]:
            copy.start()

    def arrived(group):
        for copy in groups[group]:
            copy.wait()
        if group + 1 < len(groups):
            begin(group + 1)

    columns = [pl.ds(k * width, width) for k in range(4)]
    begin(0)
    arrived(0)
    for step in range(tiles):
        for k in range(4):
            hold_a[step, :, columns[k]] = silu(mul(rows[step], first[k]))
    now, later = hold_a, hold_b
    for layer in range(layers):
        arrived(1 + layer)
        for step in range(tiles):
            for k in range(4):
                later[step, :, columns[k]] = silu(mul(now[step], middle[k, layer]))
        now, later = later, now
    arrived(1 + layers)
    matrix = last[...].reshape(out_ref.shape[1], now.shape[2])
    for step in range(tiles):
        result[step] = mul_nt(now[step], matrix).astype(BF16)
        outgoing[step].start()
    for copy in outgoing:
        copy.wait()


def call(kernel, out, *args, passed=(), scratch=(), flops=0, specs=None, outs=None, aliases=None, limit=VMEM_LIMIT):
    size = sum(a.size * a.dtype.itemsize for a in args)
    size += sum(o.size * o.dtype.itemsize for o in out)
    vmem = pl.BlockSpec(memory_space=pltpu.VMEM)
    return pl.pallas_call(
        kernel,
        out_shape=[jax.ShapeDtypeStruct(o.shape, o.dtype) for o in out],
        in_specs=(specs or [vmem] * len(args)) + [pl.BlockSpec(memory_space=pl.ANY)] * len(passed),
        out_specs=outs or [vmem] * len(out),
        scratch_shapes=scratch,
        input_output_aliases=aliases or {},
        compiler_params=pltpu.CompilerParams(vmem_limit_bytes=limit),
        cost_estimate=pl.CostEstimate(flops=flops, bytes_accessed=size, transcendentals=0),
    )(*args, *passed)


def ring(count, step):
    return [(i, (i + step) % count) for i in range(count)]


def exchange(north, south):
    total = lax.axis_size(DEVICE_AXES)
    below = lax.ppermute(north, DEVICE_AXES, ring(total, 1))
    above = lax.ppermute(south, DEVICE_AXES, ring(total, -1))
    return below, above


def from_sides(*shards):
    below = [lax.ppermute(x, "sec", ring(4, 1)) for x in shards]
    above = [lax.ppermute(x, "sec", ring(4, -1)) for x in shards]
    return below, above


def from_far(below, above):
    return lax.ppermute(below, "sec", ring(4, 1)), lax.ppermute(above, "sec", ring(4, -1))


def on_device(
    fields, neighbours, operator, rates, regime_ids, input_proj, hidden_proj, output_proj
):
    count, points, width = fields.shape
    rows_dev = count * points
    groups = lax.axis_size("elem")
    capacity = 2 * rows_dev // groups
    slots = groups * capacity
    shape = jax.ShapeDtypeStruct
    nbt = neighbours.T
    ids = regime_ids.T

    mine = (input_proj[0], output_proj[0].T)
    below, above = from_sides(*mine)
    first, last = ([m, a, None, b] for m, a, b in zip(mine, above, below))
    ends_far = from_far(below[0], above[1])
    anywhere = pl.BlockSpec(memory_space=pl.ANY)
    vmem = pl.BlockSpec(memory_space=pltpu.VMEM)

    edge = shape((count * SIDE, width), BF16)
    inner = shape((rows_dev, width), F32)
    start = fields.reshape(rows_dev, width)
    north, south = call(
        start_edge_kernel, [edge] * 2, start, nbt, operator, rates,
        scratch=[
            pltpu.VMEM((rows_dev, width), F32),
            pltpu.VMEM(nbt.shape, jnp.int32),
            pltpu.VMEM(operator.shape, F32),
            pltpu.VMEM(rates.shape, F32),
            pltpu.SemaphoreType.DMA((4,)),
        ],
        specs=[anywhere] * 4,
        limit=58 * 1024 * 1024,
        flops=2 * 10**9,
    )
    prev, next_ = exchange(north, south)
    second, pick = call(
        functools.partial(start_kernel, capacity, groups),
        [inner, shape((slots, rows_dev), BF16)],
        start, nbt, operator, rates, ids, flops=3 * 10**9,
    )
    step_args = (second, prev, next_, nbt, operator, rates)
    north, south = call(
        step_edge_kernel, [edge] * 2, *step_args, passed=(below[0], above[0]), flops=2 * 10**9
    )
    (second,) = call(step_kernel, [inner], *step_args, flops=3 * 10**9)
    prev, next_ = exchange(north, south)
    state, outgoing, *layer = call(
        send_kernel,
        [
            shape((rows_dev, width), F32),
            shape((slots, width), BF16),
            *[shape(hidden_proj.shape[2:], BF16)] * 2,
        ],
        second, prev, next_, nbt, pick, hidden_proj[0],
        passed=(below[1], above[1]),
        specs=[vmem] * 5 + [anywhere],
        outs=[vmem] * 2 + [anywhere] * 2,
        scratch=[pltpu.SemaphoreType.DMA((2,))],
        flops=3 * 10**9,
    )
    hidden_below, hidden_above = from_sides(*layer)
    low_below, low_above = call(
        pass_kernel, [layer[0]] * 2, hidden_below[0], hidden_above[0],
        specs=[anywhere] * 2, outs=[anywhere] * 2, aliases={0: 0, 1: 1}, limit=58 * 1024 * 1024, flops=19 * 10**9,
    )
    far = from_far(low_below, hidden_above[1])
    first[2], last[2] = call(
        pass_kernel, ends_far, *ends_far,
        specs=[anywhere] * 2, outs=[anywhere] * 2, aliases={0: 0, 1: 1}, limit=58 * 1024 * 1024, flops=10 * 10**9,
    )
    incoming = lax.all_to_all(
        outgoing.reshape(groups, capacity, width), "elem", split_axis=0, concat_axis=0, tiled=True
    )
    hid = hidden_proj.shape[2]
    tile = 512
    sec = lax.axis_index("sec").astype(jnp.int32).reshape(1)
    (result,) = call(
        functools.partial(network_kernel, tile),
        [shape((slots, width), BF16)],
        sec, incoming.reshape(slots, width), *first, hidden_proj[0], low_above, hidden_above[1], *far, low_below, hidden_below[1], *last,
        scratch=[
            pltpu.VMEM((4, *input_proj.shape[1:2], hid // 4), BF16),
            pltpu.VMEM((4, *hidden_proj.shape[1:3], hid // 4), BF16),
            pltpu.VMEM((4, width // 4, hid), BF16),
            pltpu.VMEM((slots // tile, tile, hid), BF16),
            pltpu.VMEM((slots // tile, tile, hid), BF16),
            pltpu.VMEM((slots // tile, tile, width), BF16),
            pltpu.VMEM((slots // tile, tile, width), BF16),
            pltpu.SemaphoreType.DMA((4, 2 + hidden_proj.shape[1])),
            pltpu.SemaphoreType.DMA((slots // tile,)),
            pltpu.SemaphoreType.DMA((slots // tile,)),
        ],
        specs=[pl.BlockSpec(memory_space=pltpu.SMEM)] + [anywhere] * 16,
        outs=[anywhere],
        limit=58 * 1024 * 1024,
        flops=7 * 10**9,
    )
    returned = lax.all_to_all(
        result.reshape(groups, capacity, width), "elem", split_axis=0, concat_axis=0, tiled=True
    )
    (updated,) = call(
        functools.partial(add_kernel, capacity, groups),
        [shape((rows_dev, width), F32)],
        state, returned.reshape(slots, width), ids, flops=10**9,
    )
    return updated.reshape(count, points, width)


def solution(mesh):
    return jax.shard_map(
        on_device,
        mesh=mesh,
        in_specs=(
            P(DEVICE_AXES, None, None),
            P(DEVICE_AXES, None),
            P(),
            P(),
            P(DEVICE_AXES, None),
            P("elem", None, "sec"),
            P("elem", None, None, "sec"),
            P("elem", None, "sec"),
        ),
        out_specs=P(DEVICE_AXES, None, None),
        check_vma=False,
    )
```
